32 devices in a mesh: clip: 2 (over x), tm: 16 (over z, y, core).
Axes of the slice: x: 2, y: 2, z: 4, core: 2. Of those that a mesh axis runs over, the one named last changes fastest.
Arguments:
- tokens: bfloat16 [32768, 512], P(('clip', 'tm')), parts along dimension 0, may hold values from -6 to 6
- qkv_weight: bfloat16 [512, 1536], replicated, may hold values from -0.25 to 0.25
- out_weight: bfloat16 [512, 1024], replicated, may hold values from -0.25 to 0.25
- conv_weight: bfloat16 [3, 3, 256, 256], replicated, may hold values from -0.125 to 0.125
- norm_gain: float32 [256], replicated, may hold values from 0.25 to 1.75
- norm_bias: float32 [256], replicated, may hold values from -3 to 3
- group_map: int32 [32], P('clip'), parts along dimension 0, may hold values from 0 to 7, as said below
- token_order: int32 [2048], P('clip'), parts along dimension 0, may hold values from 0 to 1023, each once
- valid_frames: int32 [32], P('clip'), parts along dimension 0, may hold values from 1 to 16
Outputs:
- decoded: bfloat16 [32, 32, 128, 256], P('clip', 'tm'), parts along dimension 0
The draws below stay inside these ranges and needn't reach their ends.
There are 2 independent parts, one for each index of `clip`. The reference program is written for one: setup_inputs(seed, part) draws one part's arguments, and reference() takes and returns one part's arrays. A program takes and returns all parts, laid end to end along the dimension named above; an argument that names none is the same for every part. Nothing has to cross between parts.
Inputs may be any that keep to these rules, and one draw needn't show every extreme that they name: `group_map`: never falls from one run to the next, and every group from 0 to 7 holds at least one run.
All inputs are finite; a program needn't handle non-finite values.
Results may differ from the reference program's by a relative error of at most 0.0055.
The reference program's roundings to bfloat16 on the way count: a program that leaves them out, or rounds other values in their place, can miss the bound.
Values may be sent and summed in bfloat16 or wider, within the bound.
No kernel may reach another device: no remote copies, remote signals or barrier semaphores. Data moves between devices by JAX's collectives and lax.ppermute only.
A program may use at most 64 MiB of HBM per device.

```python
import jax
import jax.numpy as jnp
from jax import lax

D = 512
HEADS = 16
C = 256
NORM_GROUPS = 32
TIME_GROUPS = 8
TOK_DEV = 1024
TOKENS = 16384
FRAMES = 16
N_TM = 16


def draw_group_map(key, part):
    cuts = jax.random.permutation(jax.random.fold_in(key, 11), N_TM - 1)[:TIME_GROUPS - 1] + 1
    positions = jnp.arange(N_TM, dtype=jnp.int32)
    return jnp.sum((positions[:, None] >= cuts[None, :]).astype(jnp.int32), axis=1).astype(jnp.int32)


def draw_valid_frames(key, part):
    lowest = FRAMES // 3
    positions = jnp.arange(N_TM, dtype=jnp.int32)
    trend = lowest + positions * (FRAMES - lowest) // max(N_TM - 1, 1)
    spread = FRAMES // 8
    jitter = jax.random.randint(jax.random.fold_in(key, 23), (N_TM,), -spread, spread + 1)
    return jnp.clip(trend + jitter, 1, FRAMES).astype(jnp.int32)


def levels(rng, dims, split, smallest, high):
    level = 1.0
    for dim, blocks in split:
        heights = jax.random.uniform(jax.random.fold_in(jax.random.fold_in(rng, 6), dim), (blocks,), jnp.float32, smallest / len(split), high / len(split))
        level = level * jnp.repeat(jnp.exp(heights), dims[dim] // blocks).reshape((-1,) + (1,) * (len(dims) - 1 - dim))
    return level


def gaussian(rng, dims, deviation, bound, pieces=(), held_as=jnp.bfloat16):
    level = levels(rng, dims, pieces, -0.22, 0.18) if pieces else 1.0
    result = jax.random.normal(rng, dims, jnp.float32) * deviation * level
    return jnp.minimum(jnp.maximum(result, -bound), bound).astype(held_as)


def setup_inputs(seed: int = 0, part: int = 0) -> dict:
    arg_keys = jax.random.split(jax.random.key(seed), 10)
    part_keys = jax.random.split(jax.random.fold_in(arg_keys[9], part), 10)
    tokens = gaussian(part_keys[0], (TOKENS, D), 1.0, 6.0, ((0, 16),))
    qkv_weight = gaussian(arg_keys[1], (D, 3 * D), D ** -0.5, 0.25)
    out_weight = gaussian(arg_keys[2], (D, 4 * C), D ** -0.5, 0.25)
    conv_weight = gaussian(arg_keys[3], (3, 3, C, C), (9 * C) ** -0.5, 0.125)
    norm_gain = jnp.clip(1.0 + 0.15 * jax.random.normal(arg_keys[4], (C,), jnp.float32), 0.25, 1.75)
    norm_bias = gaussian(arg_keys[5], (C,), 0.5, 3.0, (), jnp.float32)
    group_map = draw_group_map(jax.random.fold_in(jax.random.fold_in(arg_keys[9], part), 71), part)
    token_order = jax.random.permutation(part_keys[7], TOK_DEV).astype(jnp.int32)
    valid_frames = draw_valid_frames(jax.random.fold_in(jax.random.fold_in(arg_keys[9], part), 71), part)
    return dict(tokens=tokens, qkv_weight=qkv_weight, out_weight=out_weight, conv_weight=conv_weight, norm_gain=norm_gain, norm_bias=norm_bias, group_map=group_map, token_order=token_order, valid_frames=valid_frames)


def reference(tokens, qkv_weight, out_weight, conv_weight, norm_gain, norm_bias, group_map, token_order, valid_frames):
    head_dim = D // HEADS
    highest = lax.Precision.HIGHEST
    spans = tokens.reshape(N_TM, TOK_DEV, D)

    def span_state(span):
        mixed = jnp.dot(span, qkv_weight, preferred_element_type=jnp.float32).astype(jnp.bfloat16)
        key_feats = jax.nn.relu(mixed[:, D:2 * D]).astype(jnp.float32).reshape(TOK_DEV, HEADS, head_dim)
        value_rows = mixed[:, 2 * D:].astype(jnp.float32).reshape(TOK_DEV, HEADS, head_dim)
        state = jnp.einsum('thk,thv->khv', key_feats, value_rows, precision=highest).reshape(head_dim, D)
        return (state, lax.optimization_barrier(jnp.sum(key_feats, axis=0)).reshape(D))
    span_states, span_sums = lax.map(span_state, spans)
    earlier = (group_map[None, :] < group_map[:, None]).astype(jnp.float32)
    prefix_states = jnp.einsum('cd,dkv->ckv', earlier, span_states, precision=highest)
    prefix_sums = jnp.dot(earlier, span_sums, precision=highest)
    inverse = jnp.argsort(token_order).astype(jnp.int32)

    def span_output(packed):
        span, state, key_total = packed
        mixed = jnp.dot(span, qkv_weight, preferred_element_type=jnp.float32).astype(jnp.bfloat16)
        query_feats = jax.nn.relu(mixed[:, :D]).astype(jnp.float32).reshape(TOK_DEV, HEADS, head_dim)
        numer = jnp.einsum('thk,khv->thv', query_feats, state.reshape(head_dim, HEADS, head_dim), precision=highest)
        denom = jnp.einsum('thk,hk->th', query_feats, key_total.reshape(HEADS, head_dim), precision=highest) + 1.0
        attended = (numer / denom[:, :, None]).reshape(TOK_DEV, D).astype(jnp.bfloat16)
        raster = jnp.take(attended, inverse, axis=0)
        return jnp.dot(raster, out_weight, preferred_element_type=jnp.float32).astype(jnp.bfloat16)
    mapped = lax.map(span_output, (spans, span_states + prefix_states, span_sums + prefix_sums))
    row_tokens = TOK_DEV // N_TM
    shuffled = mapped.reshape(N_TM, N_TM, row_tokens, 2, 2, C).transpose(0, 1, 3, 2, 4, 5)
    shuffled = shuffled.reshape(N_TM, 2 * N_TM, 2 * row_tokens, C)
    row_tile = jnp.arange(2 * N_TM, dtype=jnp.int32) // 2
    frame_ids = jnp.arange(N_TM, dtype=jnp.int32)
    frame_mask = (frame_ids[:, None] < jnp.take(valid_frames, row_tile)[None, :])[:, :, None, None]
    shuffled = jnp.where(frame_mask, shuffled, jnp.zeros((), jnp.bfloat16))
    convolved = lax.conv_general_dilated(shuffled, conv_weight, (1, 1), ((1, 1), (1, 1)), dimension_numbers=('NHWC', 'HWIO', 'NHWC'), preferred_element_type=jnp.float32)
    convolved = jnp.where(frame_mask, convolved, jnp.zeros((), jnp.float32))
    group_size = C // NORM_GROUPS
    total_count = jnp.sum(valid_frames).astype(jnp.float32) * (group_size * 4 * row_tokens)

    def group_total(field):
        return lax.optimization_barrier(jnp.sum(field, axis=(0, 1, 2))).reshape(NORM_GROUPS, group_size).sum(axis=1)
    group_mean = group_total(convolved) / total_count
    centred = jnp.where(frame_mask, convolved - jnp.repeat(group_mean, group_size), jnp.zeros((), jnp.float32))
    group_var = group_total(centred * centred) / total_count
    norm_scale = norm_gain * lax.rsqrt(jnp.repeat(group_var, group_size) + 1e-05)
    normed = centred * norm_scale + norm_bias
    decoded = jnp.where(frame_mask, jax.nn.silu(normed), jnp.zeros((), jnp.float32))
    return decoded.astype(jnp.bfloat16)
```

```python
import functools

import jax
import jax.numpy as jnp
from jax import lax
from jax.experimental import pallas as pl
from jax.experimental.pallas import tpu as pltpu
from jax.sharding import PartitionSpec as P

HEADS = 16
NORM_GROUPS = 32
BF = jnp.bfloat16
F32 = jnp.float32
MIB = 1024 * 1024


def dot(a, b, **kw):
    return jnp.dot(a, b, preferred_element_type=F32, **kw)


def params(mib, dims=1):
    return pltpu.CompilerParams(
        vmem_limit_bytes=mib * MIB, dimension_semantics=("arbitrary",) * dims
    )


def cost(flops, nbytes, trans=0):
    return pl.CostEstimate(flops=int(flops), bytes_accessed=int(nbytes), transcendentals=int(trans))


def same_block(shape, size):
    rows = lax.broadcasted_iota(jnp.int32, shape, 0) // size
    cols = lax.broadcasted_iota(jnp.int32, shape, 1) // size
    return rows == cols


def permute_kernel(order_ref, tok_ref, out_ref):
    rows, count = out_ref.shape[0], tok_ref.shape[0]
    place = lax.broadcasted_iota(jnp.int32, (rows, count), 0) + pl.program_id(0) * rows
    pick = jnp.where(place == order_ref[...], 1.0, 0.0).astype(BF)
    out_ref[...] = dot(pick, tok_ref[...]).astype(BF)


def permute(order, tokens):
    count, width = tokens.shape
    steps = 2
    return pl.pallas_call(
        permute_kernel,
        grid=(steps,),
        in_specs=[
            pl.BlockSpec((1, count), lambda i: (0, 0)),
            pl.BlockSpec((count, width), lambda i: (0, 0)),
        ],
        out_specs=pl.BlockSpec((count // steps, width), lambda i: (i, 0)),
        out_shape=jax.ShapeDtypeStruct((count, width), BF),
        compiler_params=params(32),
        cost_estimate=cost(2 * count * count * width, 4 * count * width),
    )(order.reshape(1, count), tokens)


def state_kernel(head, tok_ref, wk_ref, wv_ref, out_ref, acc_ref, sum_ref):
    step = pl.program_id(0)
    width = tok_ref.shape[1]
    block = acc_ref.shape[1]

    @pl.when(step == 0)
    def _():
        acc_ref[...] = jnp.zeros_like(acc_ref)
        sum_ref[...] = jnp.zeros_like(sum_ref)

    tok = tok_ref[...]
    keys = jnp.maximum(dot(tok, wk_ref[...]), 0.0)
    keys_b = keys.astype(BF)
    vals_b = dot(tok, wv_ref[...]).astype(BF)
    sum_ref[0:1, :] += jnp.sum(keys_b.astype(F32), axis=0, keepdims=True)
    for i in range(width // block):
        cut = slice(i * block, (i + 1) * block)
        acc_ref[i] += lax.dot_general(
            keys_b[:, cut], vals_b[:, cut], (((0,), (0,)), ((), ())), preferred_element_type=F32
        )

    @pl.when(step == pl.num_programs(0) - 1)
    def _():
        own = same_block((block, block), head)
        parts = []
        for i in range(width // block):
            full = jnp.where(own, acc_ref[i], 0.0)
            small = full[:head]
            for h in range(1, block // head):
                small = small + full[h * head : (h + 1) * head]
            parts.append(small)
        total = sum_ref[0:1, :]
        high = total.astype(BF).astype(F32)
        low = total - high
        out_ref[0] = jnp.concatenate(
            [
                jnp.concatenate(parts, axis=1),
                high,
                low,
                jnp.zeros((out_ref.shape[1] - head - 2, width), F32),
            ],
            axis=0,
        ).astype(BF)


def run_state(tokens, qkv_weight, head):
    count, width = tokens.shape
    steps, block = 4, 256
    rows = head + 16
    return pl.pallas_call(
        functools.partial(state_kernel, head),
        grid=(steps,),
        in_specs=[
            pl.BlockSpec((count // steps, width), lambda i: (i, 0)),
            pl.BlockSpec((width, width), lambda i: (0, 1)),
            pl.BlockSpec((width, width), lambda i: (0, 2)),
        ],
        out_specs=pl.BlockSpec((1, rows, width), lambda i: (0, 0, 0)),
        out_shape=jax.ShapeDtypeStruct((1, rows, width), BF),
        scratch_shapes=[
            pltpu.VMEM((width // block, block, block), F32),
            pltpu.VMEM((8, width), F32),
        ],
        compiler_params=params(32),
        cost_estimate=cost(4 * count * width * width, 8 * count * width),
    )(tokens, qkv_weight, qkv_weight)


def queries(tok, wq):
    return jnp.maximum(dot(tok, wq).astype(BF).astype(F32), 0.0)


def attend(qf, state, total, own, ones):
    block = own.shape[0]
    head, width = state.shape
    qb = qf.astype(BF)
    den_in = (qf * total).astype(BF)
    outs = []
    for i in range(width // block):
        cut = slice(i * block, (i + 1) * block)
        wide = jnp.concatenate([state[:, cut]] * (block // head), axis=0)
        wide = jnp.where(own, wide, jnp.zeros_like(wide))
        numer = dot(qb[:, cut], wide)
        denom = dot(den_in[:, cut], ones) + 1.0
        outs.append(numer / denom)
    return jnp.concatenate(outs, axis=1)


def valid_rows(first, limit, frames, rows):
    frame = lax.broadcasted_iota(jnp.int32, (frames * rows, 1), 0) // rows + first
    return frame < limit


def near_kernel(
    order, rows, pos_ref, group_ref, valid_ref,
    buf_ref, own_ref, inner_ref, wq_ref, wo_ref,
    pown_ref, pinner_ref, state_ref, total_ref,
    acc_ref, pend_ref, att_ref,
):
    step = pl.program_id(0)
    width = own_ref.shape[1]
    frames = own_ref.shape[0] // rows
    me = pos_ref[0]
    head = state_ref.shape[1]

    @pl.when(step == 0)
    def _():
        acc_ref[...] = jnp.zeros_like(acc_ref)
        pend_ref[...] = jnp.zeros_like(pend_ref)

    block = 256
    own = same_block((block, block), head)
    ones = jnp.where(own, 1.0, 0.0).astype(BF)
    wq = wq_ref[...]
    q_own = queries(own_ref[...], wq)
    q_inner = queries(inner_ref[...], wq)
    for i in range(frames):
        frame = step * frames + i
        rel = jnp.bitwise_xor(frame, me)
        slot = jnp.int32(0)
        for bit, k in enumerate(order):
            slot = slot + (jnp.bitwise_and(rel, k) // k) * (1 << bit)
        piece = buf_ref[slot].astype(F32)
        before = group_ref[jnp.maximum(frame - 1, 0)]
        fresh = jnp.where(group_ref[frame] != before, 1.0, 0.0)
        pend = pend_ref[...]
        acc = acc_ref[...] + fresh * pend
        acc_ref[...] = acc
        pend_ref[...] = (1.0 - fresh) * pend + piece
        summed = acc + piece
        state = summed[:head].astype(BF)
        total = summed[head : head + 1] + summed[head + 1 : head + 2]
        state_ref[i] = state
        total_ref[i] = jnp.broadcast_to(total, (8, width))
        cut = slice(i * rows, (i + 1) * rows)
        both = jnp.concatenate([q_own[cut], q_inner[cut]], axis=0)
        res = attend(both, state, total, own, ones)
        att_ref[0, cut] = res[:rows]
        att_ref[1, cut] = res[rows:]
    first = step * frames
    keep_own = valid_rows(first, valid_ref[me], frames, rows)
    keep_inner = valid_rows(first, valid_ref[jnp.bitwise_xor(me, 1)], frames, rows)
    half = wo_ref.shape[1] // 2
    wo = wo_ref[...]
    odd = (me % 2) == 1
    p_own = dot(att_ref[0].astype(BF), wo)
    pown_ref[...] = jnp.where(keep_own, p_own, 0.0).astype(BF)
    w_in = jnp.where(odd, wo[:, half:], wo[:, :half])
    p_in = dot(att_ref[1].astype(BF), w_in)
    pinner_ref[...] = jnp.where(keep_inner, p_in, 0.0).astype(BF)


def near(order, rows, me, group_map, valid, buf, own, inner, qkv_weight, out_weight, head):
    count, width = own.shape
    frames = 4
    steps = count // rows // frames
    wide = out_weight.shape[1]
    m = frames * rows
    n, deep, _ = buf.shape
    whole = lambda *shape: pl.BlockSpec(shape, lambda i, *_: (0,) * len(shape))
    return pl.pallas_call(
        functools.partial(near_kernel, order, rows),
        grid_spec=pltpu.PrefetchScalarGridSpec(
            num_scalar_prefetch=3,
            grid=(steps,),
            in_specs=[
                whole(n, deep, width),
                pl.BlockSpec((m, width), lambda i, *_: (i, 0)),
                pl.BlockSpec((m, width), lambda i, *_: (i, 0)),
                pl.BlockSpec((width, width), lambda i, *_: (0, 0)),
                whole(width, wide),
            ],
            out_specs=[
                pl.BlockSpec((m, wide), lambda i, *_: (i, 0)),
                pl.BlockSpec((m, wide // 2), lambda i, *_: (i, 0)),
                pl.BlockSpec((frames, head, width), lambda i, *_: (i, 0, 0)),
                pl.BlockSpec((frames, 8, width), lambda i, *_: (i, 0, 0)),
            ],
            scratch_shapes=[
                pltpu.VMEM((deep, width), F32),
                pltpu.VMEM((deep, width), F32),
                pltpu.VMEM((2, m, width), F32),
            ],
        ),
        out_shape=[
            jax.ShapeDtypeStruct((count, wide), BF),
            jax.ShapeDtypeStruct((count, wide // 2), BF),
            jax.ShapeDtypeStruct((n, head, width), BF),
            jax.ShapeDtypeStruct((n, 8, width), F32),
        ],
        compiler_params=params(40),
        cost_estimate=cost(12 * count * width * width, 16 * count * width),
    )(me, group_map, valid, buf, own, inner, qkv_weight, out_weight)


def conv_kernel(
    rows, pos_ref, valid_ref,
    outer_ref, state_ref, total_ref, pown_ref, pinner_ref, wq_ref, wo_ref, wc_ref,
    conv_ref, stat_ref,
    x_ref, att_ref, run_ref,
):
    step = pl.program_id(0)
    m = outer_ref.shape[0]
    frames = m // rows
    me = pos_ref[0]
    odd = (me % 2) == 1
    channels = conv_ref.shape[3]
    head = state_ref.shape[1]
    block = 256
    own = same_block((block, block), head)
    ones = jnp.where(own, 1.0, 0.0).astype(BF)
    qf = queries(outer_ref[...], wq_ref[...])
    for i in range(frames):
        cut = slice(i * rows, (i + 1) * rows)
        att_ref[cut] = attend(qf[cut], state_ref[i], total_ref[i][0:1], own, ones)
    first = step * frames
    outer_at = jnp.clip(me + jnp.where(odd, 1, -1), 0, valid_ref.shape[0] - 1)
    keep = valid_rows(first, valid_ref[outer_at], frames, rows)
    half = wo_ref.shape[1] // 2
    wo = wo_ref[...]
    w_out = jnp.where(odd, wo[:, :half], wo[:, half:])
    far = jnp.where(keep, dot(att_ref[...].astype(BF), w_out), 0.0)
    close = pinner_ref[...].astype(F32)
    mine = pown_ref[...].astype(F32)
    lines = [
        jnp.where(odd, close, far),
        mine[:, :half],
        mine[:, half:],
        jnp.where(odd, far, close),
    ]
    column = lax.broadcasted_iota(jnp.int32, (m, 1), 0) % rows
    for r, line in enumerate(lines):
        even_px, odd_px = line[:, :channels], line[:, channels:]
        left = jnp.where(column == 0, 0.0, pltpu.roll(odd_px, 1, 0))
        right = jnp.where(column == rows - 1, 0.0, pltpu.roll(even_px, m - 1, 0))
        at = 3 * r * channels
        for b, taps in enumerate(((left, even_px, odd_px), (even_px, odd_px, right))):
            for d, tap in enumerate(taps):
                x_ref[b * m : (b + 1) * m, at + d * channels : at + (d + 1) * channels] = tap.astype(BF)
    deep = wc_ref.shape[0]
    limit = valid_ref[me]
    live = valid_rows(first, limit, frames, rows)
    live2 = jnp.concatenate([live, live], axis=0)
    outs = []
    for y in range(2):
        at = 3 * y * channels
        res = jnp.where(live2, dot(x_ref[:, at : at + deep], wc_ref[...]), 0.0)
        conv_ref[y, 0] = res[:m]
        conv_ref[y, 1] = res[m:]
        outs.append(res)
    part = jnp.sum(outs[0] + outs[1], axis=0, keepdims=True)
    count = (jnp.clip(limit - first, 0, frames) * (4 * rows)).astype(F32)
    mean = part / jnp.maximum(count, 1.0)
    dev = [jnp.where(live2, o - mean, 0.0) for o in outs]
    spread = jnp.sum(dev[0] * dev[0] + dev[1] * dev[1], axis=0, keepdims=True)

    @pl.when(step == 0)
    def _():
        run_ref[...] = jnp.zeros_like(run_ref)

    had = (jnp.clip(limit, 0, first) * (4 * rows)).astype(F32)
    run_sum = run_ref[0:1, :]
    gap = mean - run_sum / jnp.maximum(had, 1.0)
    weight = had * count / jnp.maximum(had + count, 1.0)
    run_ref[1:2, :] += spread + gap * gap * weight
    run_ref[0:1, :] = run_sum + part

    @pl.when(step == pl.num_programs(0) - 1)
    def _():
        stat_ref[...] = jnp.broadcast_to(run_ref[...][None], stat_ref.shape)


def conv(rows, me, valid, outer, state, total, pown, pinner, qkv_weight, out_weight, taps):
    count, width = outer.shape
    channels = taps.shape[1]
    frames = 4
    n = count // rows
    steps = n // frames
    m = frames * rows
    wide = out_weight.shape[1]
    head = state.shape[1]
    whole = lambda *shape: pl.BlockSpec(shape, lambda i, *_: (0,) * len(shape))
    return pl.pallas_call(
        functools.partial(conv_kernel, rows),
        grid_spec=pltpu.PrefetchScalarGridSpec(
            num_scalar_prefetch=2,
            grid=(steps,),
            in_specs=[
                pl.BlockSpec((m, width), lambda i, *_: (i, 0)),
                pl.BlockSpec((frames, head, width), lambda i, *_: (i, 0, 0)),
                pl.BlockSpec((frames, 8, width), lambda i, *_: (i, 0, 0)),
                pl.BlockSpec((m, wide), lambda i, *_: (i, 0)),
                pl.BlockSpec((m, wide // 2), lambda i, *_: (i, 0)),
                pl.BlockSpec((width, width), lambda i, *_: (0, 0)),
                whole(width, wide),
                whole(*taps.shape),
            ],
            out_specs=[
                pl.BlockSpec((2, 2, m, channels), lambda i, *_: (0, 0, i, 0)),
                whole(n, 8, channels),
            ],
            scratch_shapes=[
                pltpu.VMEM((2 * m, 12 * channels), BF),
                pltpu.VMEM((m, width), F32),
                pltpu.VMEM((8, channels), F32),
            ],
        ),
        out_shape=[
            jax.ShapeDtypeStruct((2, 2, count, channels), F32),
            jax.ShapeDtypeStruct((n, 8, channels), F32),
        ],
        compiler_params=params(40),
        cost_estimate=cost(80 * count * channels * channels, 30 * count * channels),
    )(me, valid, outer, state, total, pown, pinner, qkv_weight, out_weight, taps)


def norm_kernel(
    rows, size, pos_ref, valid_ref, stat_ref, count_ref, gain_ref, bias_ref, conv_ref,
    out_ref, mean_ref, scale_ref, mix_ref,
):
    step = pl.program_id(0)
    channels = conv_ref.shape[3]
    m = conv_ref.shape[2]
    frames = m // rows

    @pl.when(step == 0)
    def _():
        stat = stat_ref[...]
        counts = count_ref[...]
        sums, spreads = stat[:, 0, :], stat[:, 1, :]
        mix = jnp.where(same_block((channels, channels), size), 1.0, 0.0)
        all_count = jnp.sum(counts, axis=0, keepdims=True) * size

        def grouped(row):
            wide = jnp.broadcast_to(row, (8, channels))
            return dot(wide, mix, precision=lax.Precision.HIGHEST)[0:1]

        mean = grouped(jnp.sum(sums, axis=0, keepdims=True)) / all_count
        gap = sums / counts - mean
        var = grouped(jnp.sum(spreads + gap * gap * counts, axis=0, keepdims=True)) / all_count
        mean_ref[...] = mean
        scale_ref[...] = gain_ref[...] * lax.rsqrt(var + 1e-5)

    live = valid_rows(step * frames, valid_ref[pos_ref[0]], frames, rows)
    mean, scale, bias = mean_ref[...], scale_ref[...], bias_ref[...]
    for y in range(2):
        for b in range(2):
            z = (conv_ref[y, b] - mean) * scale + bias
            half = 0.5 * z
            z = half + half * jnp.tanh(half)
            z = jnp.where(live, z, 0.0)
            for c in range(channels // 128):
                mix_ref[y, c, pl.ds(b, m, 2), :] = z[:, 128 * c : 128 * (c + 1)]
    for y in range(2):
        for f in range(frames):
            for c in range(channels // 128):
                out_ref[f, y, :, 128 * c : 128 * (c + 1)] = mix_ref[
                    y, c, 2 * rows * f : 2 * rows * (f + 1), :
                ].astype(BF)


def norm(rows, me, valid, stat, counts, gain, bias, planes):
    channels = planes.shape[3]
    n = valid.shape[0]
    frames = 4
    m = frames * rows
    whole = lambda *shape: pl.BlockSpec(shape, lambda i, *_: (0,) * len(shape))
    return pl.pallas_call(
        functools.partial(norm_kernel, rows, channels // NORM_GROUPS),
        grid_spec=pltpu.PrefetchScalarGridSpec(
            num_scalar_prefetch=2,
            grid=(n // frames,),
            in_specs=[
                whole(*stat.shape),
                whole(n, channels),
                whole(1, channels),
                whole(1, channels),
                pl.BlockSpec((2, 2, m, channels), lambda i, *_: (0, 0, i, 0)),
            ],
            out_specs=pl.BlockSpec((frames, 2, 2 * rows, channels), lambda i, *_: (i, 0, 0, 0)),
            scratch_shapes=[
                pltpu.VMEM((1, channels), F32),
                pltpu.VMEM((1, channels), F32),
                pltpu.VMEM((2, channels // 128, 2 * m, 128), F32),
            ],
        ),
        out_shape=jax.ShapeDtypeStruct((n, 2, 2 * rows, channels), BF),
        compiler_params=params(32),
        cost_estimate=cost(8 * planes.size, 6 * planes.size, planes.size),
    )(me, valid, stat, counts, gain.reshape(1, channels), bias.reshape(1, channels), planes)


def local(
    tokens,
    qkv_weight,
    out_weight,
    conv_weight,
    norm_gain,
    norm_bias,
    group_map,
    token_order,
    valid_frames,
):
    tiles = lax.axis_size("tm")
    rank = lax.axis_index("tm")
    count, width = tokens.shape
    rows = count // tiles
    channels = conv_weight.shape[3]
    head = width // HEADS
    me = rank.reshape(1).astype(jnp.int32)

    def swap(x, pairs):
        return lax.ppermute(x, "tm", pairs)

    raster = permute(token_order, tokens)
    tile = lax.all_to_all(
        raster.reshape(tiles, rows, width), "tm", split_axis=0, concat_axis=0, tiled=True
    ).reshape(count, width)
    buf = run_state(tokens, qkv_weight, head)
    order = []
    k = tiles // 2
    while k >= 1:
        order.append(k)
        k //= 2
    for k in order:
        buf = jnp.concatenate([buf, swap(buf, [(i, i ^ k) for i in range(tiles)])], axis=0)
    inner = swap(tile, [(i, i ^ 1) for i in range(tiles)])
    ends = [(i, i + 1) for i in range(1, tiles - 1, 2)]
    outer = swap(tile, ends + [(j, i) for i, j in ends])
    pown, pinner, state, total = near(
        order, rows, me, group_map, valid_frames, buf, tile, inner, qkv_weight, out_weight, head
    )
    planes, stat = conv(
        rows, me, valid_frames, outer, state, total, pown, pinner, qkv_weight, out_weight,
        conv_weight.reshape(-1, channels),
    )
    stat = lax.all_to_all(stat, "tm", split_axis=0, concat_axis=0, tiled=True)
    counts = jnp.broadcast_to(
        (valid_frames * (4 * rows)).astype(F32)[:, None], (tiles, channels)
    )
    return norm(rows, me, valid_frames, stat, counts, norm_gain, norm_bias, planes)


def solution(mesh):
    in_specs = (P(("clip", "tm"), None), P(), P(), P(), P(), P(), P("clip"), P("clip"), P("clip"))
    out_specs = P("clip", "tm", None, None)
    return jax.shard_map(local, mesh=mesh, in_specs=in_specs, out_specs=out_specs, check_vma=False)
```

```python
import functools

import jax
import jax.numpy as jnp
from jax import lax
from jax.experimental import pallas as pl
from jax.experimental.pallas import tpu as pltpu
from jax.sharding import PartitionSpec as P

HEADS = 16
NORM_GROUPS = 32
BF = jnp.bfloat16
F32 = jnp.float32
MIB = 1024 * 1024
VMEM = 60


def dot(a, b, **kw):
    return jnp.dot(a, b, preferred_element_type=F32, **kw)


def params(mib, dims=1):
    return pltpu.CompilerParams(
        vmem_limit_bytes=mib * MIB, dimension_semantics=("arbitrary",) * dims
    )


def cost(flops, nbytes, trans=0):
    return pl.CostEstimate(flops=int(flops), bytes_accessed=int(nbytes), transcendentals=int(trans))


def same_block(shape, size):
    rows = lax.broadcasted_iota(jnp.int32, shape, 0) // size
    cols = lax.broadcasted_iota(jnp.int32, shape, 1) // size
    return rows == cols


def permute_kernel(order_ref, tok_ref, out_ref, pick_ref):
    count = tok_ref.shape[0]

    @pl.when(pl.program_id(0) == 0)
    def _():
        place = lax.broadcasted_iota(jnp.int32, (count, count), 0)
        pick_ref[...] = jnp.where(place == order_ref[...], 1.0, 0.0).astype(BF)

    out_ref[...] = dot(pick_ref[...], tok_ref[...]).astype(BF)


def permute(order, tokens):
    count, width = tokens.shape
    block = 256
    return pl.pallas_call(
        permute_kernel,
        grid=(width // block,),
        in_specs=[
            pl.BlockSpec((1, count), lambda i: (0, 0)),
            pl.BlockSpec((count, block), lambda i: (0, i)),
        ],
        out_specs=pl.BlockSpec((count, block), lambda i: (0, i)),
        out_shape=jax.ShapeDtypeStruct((count, width), BF),
        scratch_shapes=[pltpu.VMEM((count, count), BF)],
        compiler_params=params(VMEM),
        cost_estimate=cost(2 * count * count * width, 4 * count * width),
    )(order.reshape(1, count), tokens)


def state_kernel(head, tok_ref, wk_ref, wv_ref, out_ref, acc_ref, sum_ref):
    step = pl.program_id(0)
    width = tok_ref.shape[1]
    block = acc_ref.shape[1]

    @pl.when(step == 0)
    def _():
        acc_ref[...] = jnp.zeros_like(acc_ref)
        sum_ref[...] = jnp.zeros_like(sum_ref)

    tok = tok_ref[...]
    keys = jnp.maximum(dot(tok, wk_ref[...]), 0.0)
    keys_b = keys.astype(BF)
    vals_b = dot(tok, wv_ref[...]).astype(BF)
    sum_ref[0:1, :] += jnp.sum(keys_b.astype(F32), axis=0, keepdims=True)
    for i in range(width // block):
        cut = slice(i * block, (i + 1) * block)
        acc_ref[i] += lax.dot_general(
            keys_b[:, cut], vals_b[:, cut], (((0,), (0,)), ((), ())), preferred_element_type=F32
        )

    @pl.when(step == pl.num_programs(0) - 1)
    def _():
        own = same_block((block, block), head)
        parts = []
        for i in range(width // block):
            full = jnp.where(own, acc_ref[i], 0.0)
            small = full[:head]
            for h in range(1, block // head):
                small = small + full[h * head : (h + 1) * head]
            parts.append(small)
        total = sum_ref[0:1, :]
        high = total.astype(BF).astype(F32)
        low = total - high
        out_ref[0] = jnp.concatenate(
            [
                jnp.concatenate(parts, axis=1),
                high,
                low,
                jnp.zeros((out_ref.shape[1] - head - 2, width), F32),
            ],
            axis=0,
        ).astype(BF)


def run_state(tokens, qkv_weight, head):
    count, width = tokens.shape
    steps, block = 4, 256
    rows = head + 16
    return pl.pallas_call(
        functools.partial(state_kernel, head),
        grid=(steps,),
        in_specs=[
            pl.BlockSpec((count // steps, width), lambda i: (i, 0)),
            pl.BlockSpec((width, width), lambda i: (0, 1)),
            pl.BlockSpec((width, width), lambda i: (0, 2)),
        ],
        out_specs=pl.BlockSpec((1, rows, width), lambda i: (0, 0, 0)),
        out_shape=jax.ShapeDtypeStruct((1, rows, width), BF),
        scratch_shapes=[
            pltpu.VMEM((width // block, block, block), F32),
            pltpu.VMEM((8, width), F32),
        ],
        compiler_params=params(VMEM),
        cost_estimate=cost(4 * count * width * width, 8 * count * width),
    )(tokens, qkv_weight, qkv_weight)


def queries(tok, wq):
    return jnp.maximum(dot(tok, wq).astype(BF).astype(F32), 0.0)


def attend(qf, state, total, own, ones):
    block = own.shape[0]
    head, width = state.shape
    qb = qf.astype(BF)
    den_in = (qf * total).astype(BF)
    outs = []
    for i in range(width // block):
        cut = slice(i * block, (i + 1) * block)
        wide = jnp.concatenate([state[:, cut]] * (block // head), axis=0)
        wide = jnp.where(own, wide, jnp.zeros_like(wide))
        numer = dot(qb[:, cut], wide)
        denom = dot(den_in[:, cut], ones) + 1.0
        outs.append(numer / denom)
    return jnp.concatenate(outs, axis=1)


def valid_rows(first, limit, frames, rows):
    frame = lax.broadcasted_iota(jnp.int32, (frames * rows, 1), 0) // rows + first
    return frame < limit


HBM = pl.BlockSpec(memory_space=pltpu.HBM)
ANY = pl.BlockSpec(memory_space=pl.ANY)
INSIDE = pl.BlockSpec(memory_space=pltpu.VMEM)


def chunk(src, dst, step, m, sem):
    at = pl.ds(pl.multiple_of(step * m, m), m)
    return pltpu.make_async_copy(src.at[at], dst.at[at], sem.at[step])


def spread_row(src, row, dst, sems):
    deep, channels = dst.shape[0] * 3 // 4, dst.shape[1] // 2
    part = src.at[pl.ds(pl.multiple_of(row * deep, deep), deep), :]
    return [
        pltpu.make_async_copy(part, dst.at[:deep, :channels], sems.at[0]),
        pltpu.make_async_copy(part, dst.at[channels:, channels:], sems.at[1]),
    ]


def clear_spread(dst):
    channels = dst.shape[1] // 2
    gap = jnp.zeros((channels, channels), BF)
    dst[3 * channels :, :channels] = gap
    dst[:channels, channels:] = gap


def store_taps(x_ref, at, line, rows):
    m, channels = line.shape[0], line.shape[1] // 2
    column = lax.broadcasted_iota(jnp.int32, (m, 1), 0) % rows
    even_px, odd_px = line[:, :channels], line[:, channels:]
    left = jnp.where(column == 0, 0.0, pltpu.roll(odd_px, 1, 0))
    right = jnp.where(column == rows - 1, 0.0, pltpu.roll(even_px, m - 1, 0))
    for b, taps in enumerate(((left, even_px, odd_px), (even_px, odd_px, right))):
        for d, tap in enumerate(taps):
            cut = slice(at + d * channels, at + (d + 1) * channels)
            x_ref[b * m : (b + 1) * m, cut] = tap.astype(BF)


def line_taps(line, rows):
    m, channels = line.shape[0], line.shape[1] // 2
    column = lax.broadcasted_iota(jnp.int32, (m, 1), 0) % rows
    even_px, odd_px = line[:, :channels], line[:, channels:]
    left = jnp.where(column == 0, 0.0, pltpu.roll(odd_px, 1, 0))
    right = jnp.where(column == rows - 1, 0.0, pltpu.roll(even_px, m - 1, 0))
    return jnp.concatenate([left.astype(BF), line.astype(BF), right.astype(BF)], axis=1)


def gather_stats(run_ref, res, live, limit, first, frames, rows):
    @pl.when(first == 0)
    def _():
        run_ref[...] = jnp.zeros_like(run_ref)

    part = jnp.sum(res, axis=0, keepdims=True)
    count = (jnp.clip(limit - first, 0, frames) * (2 * rows)).astype(F32)
    mean = part / jnp.maximum(count, 1.0)
    dev = jnp.where(live, res - mean, 0.0)
    spread = jnp.sum(dev * dev, axis=0, keepdims=True)
    had = (jnp.clip(limit, 0, first) * (2 * rows)).astype(F32)
    run_sum = run_ref[0:1, :]
    gap = mean - run_sum / jnp.maximum(had, 1.0)
    weight = had * count / jnp.maximum(had + count, 1.0)
    run_ref[1:2, :] += spread + gap * gap * weight
    run_ref[0:1, :] = run_sum + part


def near_kernel(
    rows, pos_ref, group_ref, valid_ref,
    buf0_ref, buf1_ref, own_any, inner_any, qkv_hbm, wo_hbm, taps_hbm,
    near_ref, part_ref, state_ref, total_ref, stat_ref,
    acc_ref, pend_ref, att_ref, x_ref, w2_ref, w1_ref, wq_ref, wo_ref, own_ref, inner_ref,
    own_sem, inner_sem, sems,
):
    step = pl.program_id(0)
    count, width = own_ref.shape
    m = near_ref.shape[1]
    frames = m // rows
    steps = count // m
    me = pos_ref[0]
    odd = jnp.bitwise_and(me, 1)
    head = state_ref.shape[1]
    channels = near_ref.shape[2]
    row = 3 * channels
    first_half = taps_hbm.at[pl.ds(pl.multiple_of(odd * row, row), 2 * row), :]
    second_half = taps_hbm.at[pl.ds(pl.multiple_of((1 - odd) * row, row), 2 * row), :]
    query_copy = pltpu.make_async_copy(qkv_hbm.at[:, pl.ds(0, width)], wq_ref, sems.at[0])
    late = [
        pltpu.make_async_copy(wo_hbm, wo_ref, sems.at[1]),
        pltpu.make_async_copy(first_half, w2_ref.at[:, :channels], sems.at[2]),
        pltpu.make_async_copy(second_half, w2_ref.at[:, channels:], sems.at[3]),
    ] + spread_row(taps_hbm, 2 * (1 - odd), w1_ref, sems.at[pl.ds(4, 2)])

    @pl.when(step == 0)
    def _():
        query_copy.start()
        for i in range(steps):
            chunk(own_any, own_ref, i, m, own_sem).start()
            chunk(inner_any, inner_ref, i, m, inner_sem).start()
            if i == 0:
                for copy in late:
                    copy.start()
        acc_ref[...] = jnp.zeros_like(acc_ref)
        pend_ref[...] = jnp.zeros_like(pend_ref)
        clear_spread(w1_ref)
        query_copy.wait()

    chunk(own_any, own_ref, step, m, own_sem).wait()
    chunk(inner_any, inner_ref, step, m, inner_sem).wait()
    here = pl.ds(pl.multiple_of(step * m, m), m)
    block = 256
    own = same_block((block, block), head)
    ones = jnp.where(own, 1.0, 0.0).astype(BF)
    wq = wq_ref[...]
    q_own = queries(own_ref[here, :], wq)
    q_inner = queries(inner_ref[here, :], wq)
    for i in range(frames):
        frame = step * frames + i
        rel = jnp.bitwise_xor(frame, me)
        slot = rel // 2
        other = jnp.bitwise_and(rel, 1) == 1
        piece = jnp.where(other, buf1_ref[slot].astype(F32), buf0_ref[slot].astype(F32))
        before = group_ref[jnp.maximum(frame - 1, 0)]
        fresh = jnp.where(group_ref[frame] != before, 1.0, 0.0)
        pend = pend_ref[...]
        acc = acc_ref[...] + fresh * pend
        acc_ref[...] = acc
        pend_ref[...] = (1.0 - fresh) * pend + piece
        summed = acc + piece
        state = summed[:head].astype(BF)
        total = summed[head : head + 1] + summed[head + 1 : head + 2]
        state_ref[frame] = state
        total_ref[frame] = jnp.broadcast_to(total, (8, width))
        cut = slice(i * rows, (i + 1) * rows)
        both = jnp.concatenate([q_own[cut], q_inner[cut]], axis=0)
        res = attend(both, state, total, own, ones)
        att_ref[0, cut] = res[:rows]
        att_ref[1, cut] = res[rows:]
    first = step * frames
    limit = valid_ref[me]
    keep_own = valid_rows(first, limit, frames, rows)
    keep_inner = valid_rows(first, valid_ref[jnp.bitwise_xor(me, 1)], frames, rows)

    @pl.when(step == 0)
    def _():
        for copy in late:
            copy.wait()

    half = 2 * channels
    mine = jnp.where(keep_own, dot(att_ref[0].astype(BF), wo_ref[...]), 0.0)
    w_close = wo_ref[:, pl.ds(pl.multiple_of(odd * half, half), half)]
    close = jnp.where(keep_inner, dot(att_ref[1].astype(BF), w_close), 0.0)
    store_taps(x_ref, 0, mine[:, : 2 * channels], rows)
    store_taps(x_ref, row, mine[:, 2 * channels :], rows)
    live = jnp.concatenate([keep_own, keep_own], axis=0)
    pair = dot(x_ref[...], w2_ref[...])
    more = dot(line_taps(close, rows), w1_ref[...])
    more = jnp.concatenate([more[:, :channels], more[:, channels:]], axis=0)
    res = jnp.where(live, pair[:, :channels] + more, 0.0)
    near_ref[0] = res[:m]
    near_ref[1] = res[m:]
    gather_stats(stat_ref, res, live, limit, first, frames, rows)
    part_ref[0, here] = pair[:m, channels:]
    part_ref[1, here] = pair[m:, channels:]


def near(rows, me, group_map, valid, buf0, buf1, own, inner, qkv_weight, out_weight, taps, head):
    count, width = own.shape
    frames = 4
    n = count // rows
    wide = out_weight.shape[1]
    channels = taps.shape[1]
    m = frames * rows
    deep = buf0.shape[1]
    return pl.pallas_call(
        functools.partial(near_kernel, rows),
        grid_spec=pltpu.PrefetchScalarGridSpec(
            num_scalar_prefetch=3,
            grid=(n // frames,),
            in_specs=[INSIDE, INSIDE, ANY, ANY, HBM, HBM, HBM],
            out_specs=[pl.BlockSpec((2, m, channels), lambda i, *_: (0, i, 0))] + [INSIDE] * 4,
            scratch_shapes=[
                pltpu.VMEM((deep, width), F32),
                pltpu.VMEM((deep, width), F32),
                pltpu.VMEM((2, m, width), F32),
                pltpu.VMEM((2 * m, 6 * channels), BF),
                pltpu.VMEM((6 * channels, 2 * channels), BF),
                pltpu.VMEM((4 * channels, 2 * channels), BF),
                pltpu.VMEM((width, width), BF),
                pltpu.VMEM((width, wide), BF),
                pltpu.VMEM((count, width), BF),
                pltpu.VMEM((count, width), BF),
                pltpu.SemaphoreType.DMA((n // frames,)),
                pltpu.SemaphoreType.DMA((n // frames,)),
                pltpu.SemaphoreType.DMA((6,)),
            ],
        ),
        out_shape=[
            pltpu.HBM((2, count, channels), F32),
            pltpu.VMEM((2, count, channels), F32),
            pltpu.VMEM((n, head, width), BF),
            pltpu.VMEM((n, 8, width), F32),
            pltpu.VMEM((8, channels), F32),
        ],
        compiler_params=params(24),
        cost_estimate=cost(12 * count * width * width, 16 * count * width),
    )(me, group_map, valid, buf0, buf1, own, inner, qkv_weight, out_weight, taps)


def far_kernel(
    rows, pos_ref, valid_ref,
    outer_any, state_ref, total_ref, part_ref, near_stat_ref, qkv_hbm, wo_hbm, taps_hbm,
    far_ref, stat_ref,
    wx_ref, att_ref, run_ref, wq_ref, wo_ref, outer_ref, outer_sem, sems,
):
    step = pl.program_id(0)
    count, width = outer_ref.shape
    _, m, channels = far_ref.shape
    frames = m // rows
    me = pos_ref[0]
    odd = jnp.bitwise_and(me, 1)
    head = state_ref.shape[1]
    half = 2 * channels
    half_at = pl.ds(pl.multiple_of((1 - odd) * half, half), half)
    copies = [
        pltpu.make_async_copy(qkv_hbm.at[:, pl.ds(0, width)], wq_ref, sems.at[0]),
        pltpu.make_async_copy(wo_hbm.at[:, half_at], wo_ref, sems.at[1]),
    ] + spread_row(taps_hbm, 2 * odd, wx_ref, sems.at[pl.ds(2, 2)])

    @pl.when(step == 0)
    def _():
        copies[0].start()
        for i in range(count // m):
            chunk(outer_any, outer_ref, i, m, outer_sem).start()
            if i == 0:
                for copy in copies[1:]:
                    copy.start()
        clear_spread(wx_ref)
        copies[0].wait()

    chunk(outer_any, outer_ref, step, m, outer_sem).wait()
    here = pl.ds(pl.multiple_of(step * m, m), m)
    block = 256
    own = same_block((block, block), head)
    ones = jnp.where(own, 1.0, 0.0).astype(BF)
    qf = queries(outer_ref[here, :], wq_ref[...])
    for i in range(frames):
        cut = slice(i * rows, (i + 1) * rows)
        frame = step * frames + i
        att_ref[cut] = attend(qf[cut], state_ref[frame], total_ref[frame][0:1], own, ones)
    first = step * frames
    outer_at = jnp.clip(me + 2 * odd - 1, 0, valid_ref.shape[0] - 1)
    keep = valid_rows(first, valid_ref[outer_at], frames, rows)

    @pl.when(step == 0)
    def _():
        for copy in copies[1:]:
            copy.wait()

    line = jnp.where(keep, dot(att_ref[...].astype(BF), wo_ref[...]), 0.0)
    more = dot(line_taps(line, rows), wx_ref[...])
    more = jnp.concatenate([more[:, :channels], more[:, channels:]], axis=0)
    limit = valid_ref[me]
    live = valid_rows(first, limit, frames, rows)
    live = jnp.concatenate([live, live], axis=0)
    part = jnp.concatenate([part_ref[0, here], part_ref[1, here]], axis=0)
    res = jnp.where(live, part + more, 0.0)
    far_ref[0] = res[:m]
    far_ref[1] = res[m:]
    gather_stats(run_ref, res, live, limit, first, frames, rows)

    @pl.when(step == pl.num_programs(0) - 1)
    def _():
        both = jnp.concatenate([near_stat_ref[0:2], run_ref[0:2], run_ref[4:8]], axis=0)
        stat_ref[...] = jnp.broadcast_to(both[None], stat_ref.shape)


def far(rows, me, valid, outer, state, total, part, near_stat, qkv_weight, out_weight, taps):
    count, width = outer.shape
    channels = taps.shape[1]
    frames = 4
    n = count // rows
    m = frames * rows
    return pl.pallas_call(
        functools.partial(far_kernel, rows),
        grid_spec=pltpu.PrefetchScalarGridSpec(
            num_scalar_prefetch=2,
            grid=(n // frames,),
            in_specs=[ANY, INSIDE, INSIDE, INSIDE, INSIDE, HBM, HBM, HBM],
            out_specs=[
                pl.BlockSpec((2, m, channels), lambda i, *_: (0, i, 0)),
                pl.BlockSpec((n, 8, channels), lambda i, *_: (0, 0, 0)),
            ],
            scratch_shapes=[
                pltpu.VMEM((4 * channels, 2 * channels), BF),
                pltpu.VMEM((m, width), F32),
                pltpu.VMEM((8, channels), F32),
                pltpu.VMEM((width, width), BF),
                pltpu.VMEM((width, 2 * channels), BF),
                pltpu.VMEM((count, width), BF),
                pltpu.SemaphoreType.DMA((n // frames,)),
                pltpu.SemaphoreType.DMA((4,)),
            ],
        ),
        out_shape=[
            pltpu.HBM((2, count, channels), F32),
            jax.ShapeDtypeStruct((n, 8, channels), F32),
        ],
        compiler_params=params(24),
        cost_estimate=cost(40 * count * channels * channels, 30 * count * channels),
    )(me, valid, outer, state, total, part, near_stat, qkv_weight, out_weight, taps)


def norm_kernel(
    rows, size, pos_ref, valid_ref, stat_ref, count_ref, gain_ref, bias_ref, near_hbm, far_hbm,
    out_ref, mean_ref, scale_ref, mix_ref, plane_ref, sems,
):
    step = pl.program_id(0)
    frames = out_ref.shape[0]
    m = frames * rows
    channels = out_ref.shape[3]
    steps = near_hbm.shape[1] // m

    def load(y, i):
        at = pl.ds(pl.multiple_of(i * m, m), m)
        src = (near_hbm, far_hbm)[y].at[:, at]
        return pltpu.make_async_copy(src, plane_ref.at[y, :, at], sems.at[y, i])

    me = pos_ref[0]
    odd = jnp.bitwise_and(me, 1)

    @pl.when(step == 0)
    def _():
        for i in range(steps):
            for y in range(2):
                load(y, i).start()
        stat = stat_ref[...]
        counts = count_ref[...]
        mix = jnp.where(same_block((channels, channels), size), 1.0, 0.0)
        all_count = jnp.sum(counts, axis=0, keepdims=True) * (2 * size)

        def grouped(row):
            wide = jnp.broadcast_to(row, (8, channels))
            return dot(wide, mix, precision=lax.Precision.HIGHEST)[0:1]

        sums = stat[:, 0, :] + stat[:, 2, :]
        mean = grouped(jnp.sum(sums, axis=0, keepdims=True)) / all_count
        gap0 = stat[:, 0, :] / counts - mean
        gap1 = stat[:, 2, :] / counts - mean
        spread = stat[:, 1, :] + stat[:, 3, :] + (gap0 * gap0 + gap1 * gap1) * counts
        var = grouped(jnp.sum(spread, axis=0, keepdims=True)) / all_count
        mean_ref[...] = mean
        scale_ref[...] = gain_ref[...] * lax.rsqrt(var + 1e-5)

    live = valid_rows(step * frames, valid_ref[me], frames, rows)
    mean, scale, bias = mean_ref[...], scale_ref[...], bias_ref[...]
    here = pl.ds(pl.multiple_of(step * m, m), m)
    for y in range(2):
        load(y, step).wait()
        line = 1 - odd if y == 0 else odd
        for b in range(2):
            z = (plane_ref[y, b, here] - mean) * scale + bias
            half = 0.5 * z
            z = jnp.where(live, half + half * jnp.tanh(half), 0.0)
            for c in range(channels // 128):
                mix_ref[y, c, pl.ds(b, m, 2), :] = z[:, 128 * c : 128 * (c + 1)]
        for f in range(frames):
            for c in range(channels // 128):
                out_ref[f, line, :, 128 * c : 128 * (c + 1)] = mix_ref[
                    y, c, 2 * rows * f : 2 * rows * (f + 1), :
                ].astype(BF)


def norm(rows, me, valid, stat, counts, gain, bias, near_plane, far_plane):
    count, channels = near_plane.shape[1:]
    n = valid.shape[0]
    frames = 4
    m = frames * rows
    whole = lambda *shape: pl.BlockSpec(shape, lambda i, *_: (0,) * len(shape))
    return pl.pallas_call(
        functools.partial(norm_kernel, rows, channels // NORM_GROUPS),
        grid_spec=pltpu.PrefetchScalarGridSpec(
            num_scalar_prefetch=2,
            grid=(n // frames,),
            in_specs=[
                whole(*stat.shape),
                whole(n, channels),
                whole(1, channels),
                whole(1, channels),
                HBM,
                HBM,
            ],
            out_specs=pl.BlockSpec((frames, 2, 2 * rows, channels), lambda i, *_: (i, 0, 0, 0)),
            scratch_shapes=[
                pltpu.VMEM((1, channels), F32),
                pltpu.VMEM((1, channels), F32),
                pltpu.VMEM((2, channels // 128, 2 * m, 128), F32),
                pltpu.VMEM((2, 2, count, channels), F32),
                pltpu.SemaphoreType.DMA((2, n // frames)),
            ],
        ),
        out_shape=jax.ShapeDtypeStruct((n, 2, 2 * rows, channels), BF),
        compiler_params=params(VMEM),
        cost_estimate=cost(32 * count * channels, 24 * count * channels, 4 * count * channels),
    )(me, valid, stat, counts, gain.reshape(1, channels), bias.reshape(1, channels), near_plane, far_plane)


def local(
    tokens,
    qkv_weight,
    out_weight,
    conv_weight,
    norm_gain,
    norm_bias,
    group_map,
    token_order,
    valid_frames,
):
    tiles = lax.axis_size("tm")
    rank = lax.axis_index("tm")
    count, width = tokens.shape
    rows = count // tiles
    channels = conv_weight.shape[3]
    head = width // HEADS
    me = rank.reshape(1).astype(jnp.int32)

    def swap(x, pairs):
        return lax.ppermute(x, "tm", pairs)

    qkv_weight, out_weight, taps = (
        pltpu.with_memory_space_constraint(w, pltpu.HBM)
        for w in (qkv_weight, out_weight, conv_weight.reshape(-1, channels))
    )
    raster = permute(token_order, tokens)
    tile = lax.all_to_all(
        raster.reshape(tiles, rows, width), "tm", split_axis=0, concat_axis=0, tiled=True
    ).reshape(count, width)
    buf = run_state(tokens, qkv_weight, head)

    def swap_by(x, k):
        return swap(x, [(i, i ^ k) for i in range(tiles)])

    k, gate = 2, None
    while k < tiles:
        ks = [k] if k == 2 or 2 * k >= tiles else [k, 2 * k, 3 * k]
        got = [swap_by(buf, j) for j in ks]
        gate = got[0]
        buf = jnp.concatenate([buf] + got, axis=0)
        k *= 2 if len(ks) == 1 else 4
    other = swap_by(buf, 1)
    tile, _ = lax.optimization_barrier((tile, gate))
    inner = swap_by(tile, 1)
    ends = [(i, i + 1) for i in range(1, tiles - 1, 2)]
    outer = swap(tile, ends + [(j, i) for i, j in ends])
    near_plane, part, state, total, near_stat = near(
        rows, me, group_map, valid_frames, buf, other, tile, inner, qkv_weight, out_weight, taps, head
    )
    far_plane, stat = far(
        rows, me, valid_frames, outer, state, total, part, near_stat, qkv_weight, out_weight, taps
    )
    stat = lax.all_to_all(stat, "tm", split_axis=0, concat_axis=0, tiled=True)
    counts = jnp.broadcast_to(
        (valid_frames * (2 * rows)).astype(F32)[:, None], (tiles, channels)
    )
    return norm(rows, me, valid_frames, stat, counts, norm_gain, norm_bias, near_plane, far_plane)


def solution(mesh):
    in_specs = (P(("clip", "tm"), None), P(), P(), P(), P(), P(), P("clip"), P("clip"), P("clip"))
    out_specs = P("clip", "tm", None, None)
    return jax.shard_map(local, mesh=mesh, in_specs=in_specs, out_specs=out_specs, check_vma=False)
```

```python
import functools

import jax
import jax.numpy as jnp
from jax import lax
from jax.experimental import pallas as pl
from jax.experimental.pallas import tpu as pltpu
from jax.sharding import PartitionSpec as P

HEADS = 16
NORM_GROUPS = 32
BF = jnp.bfloat16
F32 = jnp.float32
MIB = 1024 * 1024
VMEM = 60


def dot(a, b, **kw):
    return jnp.dot(a, b, preferred_element_type=F32, **kw)


def params(mib, dims=1):
    return pltpu.CompilerParams(
        vmem_limit_bytes=mib * MIB, dimension_semantics=("arbitrary",) * dims
    )


def cost(flops, nbytes, trans=0):
    return pl.CostEstimate(flops=int(flops), bytes_accessed=int(nbytes), transcendentals=int(trans))


def same_block(shape, size):
    rows = lax.broadcasted_iota(jnp.int32, shape, 0) // size
    cols = lax.broadcasted_iota(jnp.int32, shape, 1) // size
    return rows == cols


def permute_kernel(order_ref, tok_ref, out_ref, pick_ref):
    count = tok_ref.shape[0]

    @pl.when(pl.program_id(0) == 0)
    def _():
        place = lax.broadcasted_iota(jnp.int32, (count, count), 0)
        pick_ref[...] = jnp.where(place == order_ref[...], 1.0, 0.0).astype(BF)

    out_ref[...] = dot(pick_ref[...], tok_ref[...]).astype(BF)


def permute(order, tokens):
    count, width = tokens.shape
    block = 256
    return pl.pallas_call(
        permute_kernel,
        grid=(width // block,),
        in_specs=[
            pl.BlockSpec((1, count), lambda i: (0, 0)),
            pl.BlockSpec((count, block), lambda i: (0, i)),
        ],
        out_specs=pl.BlockSpec((count, block), lambda i: (0, i)),
        out_shape=jax.ShapeDtypeStruct((count, width), BF),
        scratch_shapes=[pltpu.VMEM((count, count), BF)],
        compiler_params=params(VMEM),
        cost_estimate=cost(2 * count * count * width, 4 * count * width),
    )(order.reshape(1, count), tokens)


def state_kernel(head, tok_ref, wk_ref, wv_ref, out_ref, acc_ref, sum_ref):
    step = pl.program_id(0)
    width = tok_ref.shape[1]
    block = acc_ref.shape[1]

    @pl.when(step == 0)
    def _():
        acc_ref[...] = jnp.zeros_like(acc_ref)
        sum_ref[...] = jnp.zeros_like(sum_ref)

    tok = tok_ref[...]
    keys = jnp.maximum(dot(tok, wk_ref[...]), 0.0)
    keys_b = keys.astype(BF)
    vals_b = dot(tok, wv_ref[...]).astype(BF)
    sum_ref[0:1, :] += jnp.sum(keys_b.astype(F32), axis=0, keepdims=True)
    for i in range(width // block):
        cut = slice(i * block, (i + 1) * block)
        acc_ref[i] += lax.dot_general(
            keys_b[:, cut], vals_b[:, cut], (((0,), (0,)), ((), ())), preferred_element_type=F32
        )

    @pl.when(step == pl.num_programs(0) - 1)
    def _():
        own = same_block((block, block), head)
        parts = []
        for i in range(width // block):
            full = jnp.where(own, acc_ref[i], 0.0)
            small = full[:head]
            for h in range(1, block // head):
                small = small + full[h * head : (h + 1) * head]
            parts.append(small)
        total = sum_ref[0:1, :]
        high = total.astype(BF).astype(F32)
        low = total - high
        out_ref[0] = jnp.concatenate(
            [
                jnp.concatenate(parts, axis=1),
                high,
                low,
                jnp.zeros((out_ref.shape[1] - head - 2, width), F32),
            ],
            axis=0,
        ).astype(BF)


def run_state(tokens, qkv_weight, head):
    count, width = tokens.shape
    steps, block = 4, 256
    rows = head + 16
    return pl.pallas_call(
        functools.partial(state_kernel, head),
        grid=(steps,),
        in_specs=[
            pl.BlockSpec((count // steps, width), lambda i: (i, 0)),
            pl.BlockSpec((width, width), lambda i: (0, 1)),
            pl.BlockSpec((width, width), lambda i: (0, 2)),
        ],
        out_specs=pl.BlockSpec((1, rows, width), lambda i: (0, 0, 0)),
        out_shape=jax.ShapeDtypeStruct((1, rows, width), BF),
        scratch_shapes=[
            pltpu.VMEM((width // block, block, block), F32),
            pltpu.VMEM((8, width), F32),
        ],
        compiler_params=params(VMEM),
        cost_estimate=cost(4 * count * width * width, 8 * count * width),
    )(tokens, qkv_weight, qkv_weight)


def queries(tok, wq):
    return jnp.maximum(dot(tok, wq).astype(BF).astype(F32), 0.0)


def attend(qf, state, total, own, ones):
    block = own.shape[0]
    head, width = state.shape
    qb = qf.astype(BF)
    den_in = (qf * total).astype(BF)
    outs = []
    for i in range(width // block):
        cut = slice(i * block, (i + 1) * block)
        wide = jnp.concatenate([state[:, cut]] * (block // head), axis=0)
        wide = jnp.where(own, wide, jnp.zeros_like(wide))
        numer = dot(qb[:, cut], wide)
        denom = dot(den_in[:, cut], ones) + 1.0
        outs.append(numer / denom)
    return jnp.concatenate(outs, axis=1)


def valid_rows(first, limit, frames, rows):
    frame = lax.broadcasted_iota(jnp.int32, (frames * rows, 1), 0) // rows + first
    return frame < limit


HBM = pl.BlockSpec(memory_space=pltpu.HBM)
ANY = pl.BlockSpec(memory_space=pl.ANY)
INSIDE = pl.BlockSpec(memory_space=pltpu.VMEM)


def chunk(src, dst, step, m, sem):
    at = pl.ds(pl.multiple_of(step * m, m), m)
    return pltpu.make_async_copy(src.at[at], dst.at[at], sem.at[step])


def spread_row(src, row, dst, sems):
    deep, channels = dst.shape[0] * 3 // 4, dst.shape[1] // 2
    part = src.at[pl.ds(pl.multiple_of(row * deep, deep), deep), :]
    return [
        pltpu.make_async_copy(part, dst.at[:deep, :channels], sems.at[0]),
        pltpu.make_async_copy(part, dst.at[channels:, channels:], sems.at[1]),
    ]


def clear_spread(dst):
    channels = dst.shape[1] // 2
    gap = jnp.zeros((channels, channels), BF)
    dst[3 * channels :, :channels] = gap
    dst[:channels, channels:] = gap


def store_taps(x_ref, at, line, rows):
    m, channels = line.shape[0], line.shape[1] // 2
    column = lax.broadcasted_iota(jnp.int32, (m, 1), 0) % rows
    even_px, odd_px = line[:, :channels], line[:, channels:]
    left = jnp.where(column == 0, 0.0, pltpu.roll(odd_px, 1, 0))
    right = jnp.where(column == rows - 1, 0.0, pltpu.roll(even_px, m - 1, 0))
    for b, taps in enumerate(((left, even_px, odd_px), (even_px, odd_px, right))):
        for d, tap in enumerate(taps):
            cut = slice(at + d * channels, at + (d + 1) * channels)
            x_ref[b * m : (b + 1) * m, cut] = tap.astype(BF)


def line_taps(line, rows):
    m, channels = line.shape[0], line.shape[1] // 2
    column = lax.broadcasted_iota(jnp.int32, (m, 1), 0) % rows
    even_px, odd_px = line[:, :channels], line[:, channels:]
    left = jnp.where(column == 0, 0.0, pltpu.roll(odd_px, 1, 0))
    right = jnp.where(column == rows - 1, 0.0, pltpu.roll(even_px, m - 1, 0))
    return jnp.concatenate([left.astype(BF), line.astype(BF), right.astype(BF)], axis=1)


def gather_stats(run_ref, res, live, limit, first, frames, rows):
    part = jnp.sum(res, axis=0, keepdims=True)
    count = (jnp.clip(limit - first, 0, frames) * (2 * rows)).astype(F32)
    mean = part / jnp.maximum(count, 1.0)
    dev = jnp.where(live, res - mean, 0.0)
    spread = jnp.sum(dev * dev, axis=0, keepdims=True)
    had = (jnp.clip(limit, 0, first) * (2 * rows)).astype(F32)
    run_sum = run_ref[0:1, :]
    gap = mean - run_sum / jnp.maximum(had, 1.0)
    weight = had * count / jnp.maximum(had + count, 1.0)
    run_ref[1:2, :] += spread + gap * gap * weight
    run_ref[0:1, :] = run_sum + part


def near_kernel(
    rows, parts, frames, pos_ref, group_ref, valid_ref, *refs
):
    pieces, refs = refs[: 2 * parts], refs[2 * parts :]
    own_any, inner_any, qkv_hbm, wo_hbm, taps_hbm, *refs = refs
    near_ref, part_ref, state_ref, total_ref, stat_ref, *refs = refs
    acc_ref, pend_ref, att_ref, x_ref, w2_ref, w1_ref, wq_ref, wo_ref, *refs = refs
    own_ref, inner_ref, buf_ref, own_sem, inner_sem, sems, piece_sem = refs
    step = pl.program_id(0)
    count, width = own_ref.shape
    m = frames * rows
    steps = count // m
    me = pos_ref[0]
    odd = jnp.bitwise_and(me, 1)
    head = state_ref.shape[1]
    channels = near_ref.shape[2]
    row = 3 * channels
    first_half = taps_hbm.at[pl.ds(pl.multiple_of(odd * row, row), 2 * row), :]
    second_half = taps_hbm.at[pl.ds(pl.multiple_of((1 - odd) * row, row), 2 * row), :]
    query_copy = pltpu.make_async_copy(qkv_hbm.at[:, pl.ds(0, width)], wq_ref, sems.at[0])
    late = [
        pltpu.make_async_copy(wo_hbm, wo_ref, sems.at[1]),
        pltpu.make_async_copy(first_half, w2_ref.at[:, :channels], sems.at[2]),
        pltpu.make_async_copy(second_half, w2_ref.at[:, channels:], sems.at[3]),
    ] + spread_row(taps_hbm, 2 * (1 - odd), w1_ref, sems.at[pl.ds(4, 2)])

    size = pieces[0].shape[0]
    fetch = [
        pltpu.make_async_copy(
            pieces[i], buf_ref.at[i // parts, pl.ds(i % parts * size, size)], piece_sem.at[i]
        )
        for i in range(2 * parts)
    ]

    @pl.when(step == 0)
    def _():
        query_copy.start()
        for copy in fetch:
            copy.start()
        for i in range(steps):
            chunk(own_any, own_ref, i, m, own_sem).start()
            chunk(inner_any, inner_ref, i, m, inner_sem).start()
            if i == 0:
                for copy in late:
                    copy.start()
        acc_ref[...] = jnp.zeros_like(acc_ref)
        pend_ref[...] = jnp.zeros_like(pend_ref)
        clear_spread(w1_ref)
        stat_ref[...] = jnp.zeros_like(stat_ref)
        query_copy.wait()
        for copy in fetch:
            copy.wait()

    chunk(own_any, own_ref, step, m, own_sem).wait()
    chunk(inner_any, inner_ref, step, m, inner_sem).wait()
    here = pl.ds(pl.multiple_of(step * m, m), m)
    block = 256
    own = same_block((block, block), head)
    ones = jnp.where(own, 1.0, 0.0).astype(BF)
    wq = wq_ref[...]
    q_own = queries(own_ref[here, :], wq)
    q_inner = queries(inner_ref[here, :], wq)
    for i in range(frames):
        frame = step * frames + i
        rel = jnp.bitwise_xor(frame, me)
        piece = buf_ref[jnp.bitwise_and(rel, 1), rel // 2].astype(F32)
        before = group_ref[jnp.maximum(frame - 1, 0)]
        fresh = jnp.where(group_ref[frame] != before, 1.0, 0.0)
        pend = pend_ref[...]
        acc = acc_ref[...] + fresh * pend
        acc_ref[...] = acc
        pend_ref[...] = (1.0 - fresh) * pend + piece
        summed = acc + piece
        state = summed[:head].astype(BF)
        total = summed[head : head + 1] + summed[head + 1 : head + 2]
        state_ref[frame] = state
        total_ref[frame] = jnp.broadcast_to(total, (8, width))
        cut = slice(i * rows, (i + 1) * rows)
        both = jnp.concatenate([q_own[cut], q_inner[cut]], axis=0)
        res = attend(both, state, total, own, ones)
        att_ref[0, cut] = res[:rows]
        att_ref[1, cut] = res[rows:]
    first = step * frames
    limit = valid_ref[me]
    keep_own = valid_rows(first, limit, frames, rows)
    keep_inner = valid_rows(first, valid_ref[jnp.bitwise_xor(me, 1)], frames, rows)

    @pl.when(step == 0)
    def _():
        for copy in late:
            copy.wait()

    half = 2 * channels
    mine = jnp.where(keep_own, dot(att_ref[0].astype(BF), wo_ref[...]), 0.0)
    w_close = wo_ref[:, pl.ds(pl.multiple_of(odd * half, half), half)]
    close = jnp.where(keep_inner, dot(att_ref[1].astype(BF), w_close), 0.0)
    store_taps(x_ref, 0, mine[:, : 2 * channels], rows)
    store_taps(x_ref, row, mine[:, 2 * channels :], rows)
    live = jnp.concatenate([keep_own, keep_own], axis=0)
    pair = dot(x_ref[...], w2_ref[...])
    more = dot(line_taps(close, rows), w1_ref[...])
    more = jnp.concatenate([more[:, :channels], more[:, channels:]], axis=0)
    res = jnp.where(live, pair[:, :channels] + more, 0.0)
    near_ref[0, here] = res[:m]
    near_ref[1, here] = res[m:]
    gather_stats(stat_ref, res, live, limit, first, frames, rows)
    part_ref[0, here] = pair[:m, channels:]
    part_ref[1, here] = pair[m:, channels:]


def near(rows, me, group_map, valid, pieces, own, inner, qkv_weight, out_weight, taps, head):
    count, width = own.shape
    frames = 16
    n = count // rows
    wide = out_weight.shape[1]
    channels = taps.shape[1]
    m = frames * rows
    deep = pieces[0].shape[1]
    parts = len(pieces) // 2
    return pl.pallas_call(
        functools.partial(near_kernel, rows, parts, frames),
        grid_spec=pltpu.PrefetchScalarGridSpec(
            num_scalar_prefetch=3,
            grid=(n // frames,),
            in_specs=[ANY] * (2 * parts + 2) + [HBM] * 3,
            out_specs=[INSIDE] * 5,
            scratch_shapes=[
                pltpu.VMEM((deep, width), F32),
                pltpu.VMEM((deep, width), F32),
                pltpu.VMEM((2, m, width), F32),
                pltpu.VMEM((2 * m, 6 * channels), BF),
                pltpu.VMEM((6 * channels, 2 * channels), BF),
                pltpu.VMEM((4 * channels, 2 * channels), BF),
                pltpu.VMEM((width, width), BF),
                pltpu.VMEM((width, wide), BF),
                pltpu.VMEM((count, width), BF),
                pltpu.VMEM((count, width), BF),
                pltpu.VMEM((2, n // 2, deep, width), BF),
                pltpu.SemaphoreType.DMA((n // frames,)),
                pltpu.SemaphoreType.DMA((n // frames,)),
                pltpu.SemaphoreType.DMA((6,)),
                pltpu.SemaphoreType.DMA((2 * parts,)),
            ],
        ),
        out_shape=[
            pltpu.VMEM((2, count, channels), F32),
            pltpu.VMEM((2, count, channels), F32),
            pltpu.VMEM((n, head, width), BF),
            pltpu.VMEM((n, 8, width), F32),
            pltpu.VMEM((8, channels), F32),
        ],
        compiler_params=params(40),
        cost_estimate=cost(1, 1),
    )(me, group_map, valid, *pieces, own, inner, qkv_weight, out_weight, taps)


def far_kernel(
    rows, first, last, pos_ref, valid_ref,
    outer_any, state_ref, total_ref, part_ref, before_ref, near_stat_ref, qkv_hbm, wo_hbm, taps_hbm,
    far_ref, stat_ref,
    wx_ref, att_ref, run_ref, wq_ref, wo_ref, outer_ref, sems,
):
    m, width = outer_ref.shape
    channels = far_ref.shape[2]
    frames = m // rows
    me = pos_ref[0]
    odd = jnp.bitwise_and(me, 1)
    head = state_ref.shape[1]
    half = 2 * channels
    half_at = pl.ds(pl.multiple_of((1 - odd) * half, half), half)
    copies = [
        pltpu.make_async_copy(qkv_hbm.at[:, pl.ds(0, width)], wq_ref, sems.at[0]),
        pltpu.make_async_copy(outer_any, outer_ref, sems.at[1]),
        pltpu.make_async_copy(wo_hbm.at[:, half_at], wo_ref, sems.at[2]),
    ] + spread_row(taps_hbm, 2 * odd, wx_ref, sems.at[pl.ds(3, 2)])
    for copy in copies:
        copy.start()
    clear_spread(wx_ref)
    run_ref[...] = before_ref[...]
    block = 256
    own = same_block((block, block), head)
    ones = jnp.where(own, 1.0, 0.0).astype(BF)
    copies[0].wait()
    copies[1].wait()
    qf = queries(outer_ref[...], wq_ref[...])
    for i in range(frames):
        cut = slice(i * rows, (i + 1) * rows)
        frame = first + i
        att_ref[cut] = attend(qf[cut], state_ref[frame], total_ref[frame][0:1], own, ones)
    outer_at = jnp.clip(me + 2 * odd - 1, 0, valid_ref.shape[0] - 1)
    keep = valid_rows(first, valid_ref[outer_at], frames, rows)
    for copy in copies[2:]:
        copy.wait()
    line = jnp.where(keep, dot(att_ref[...].astype(BF), wo_ref[...]), 0.0)
    more = dot(line_taps(line, rows), wx_ref[...])
    more = jnp.concatenate([more[:, :channels], more[:, channels:]], axis=0)
    limit = valid_ref[me]
    live = valid_rows(first, limit, frames, rows)
    live = jnp.concatenate([live, live], axis=0)
    here = pl.ds(first * rows, m)
    part = jnp.concatenate([part_ref[0, here], part_ref[1, here]], axis=0)
    res = jnp.where(live, part + more, 0.0)
    far_ref[0] = res[:m]
    far_ref[1] = res[m:]
    gather_stats(run_ref, res, live, limit, first, frames, rows)
    if last:
        both = jnp.concatenate([near_stat_ref[0:2], run_ref[0:2], run_ref[4:8]], axis=0)
        stat_ref[...] = jnp.broadcast_to(both[None], stat_ref.shape)
    else:
        stat_ref[...] = run_ref[...]


def far(rows, first, me, valid, outer, state, total, part, before, near_stat, qkv_weight, out_weight, taps):
    m, width = outer.shape
    channels = taps.shape[1]
    n = state.shape[0]
    last = first + m // rows == n
    smem = pl.BlockSpec(memory_space=pltpu.SMEM)
    stat = jax.ShapeDtypeStruct((n, 8, channels), F32) if last else pltpu.VMEM((8, channels), F32)
    return pl.pallas_call(
        functools.partial(far_kernel, rows, first, last),
        in_specs=[smem, smem, ANY] + [INSIDE] * 5 + [HBM] * 3,
        out_specs=[INSIDE, INSIDE],
        scratch_shapes=[
            pltpu.VMEM((4 * channels, 2 * channels), BF),
            pltpu.VMEM((m, width), F32),
            pltpu.VMEM((8, channels), F32),
            pltpu.VMEM((width, width), BF),
            pltpu.VMEM((width, 2 * channels), BF),
            pltpu.VMEM((m, width), BF),
            pltpu.SemaphoreType.DMA((5,)),
        ],
        out_shape=[pltpu.VMEM((2, m, channels), F32), stat],
        compiler_params=pltpu.CompilerParams(vmem_limit_bytes=32 * MIB),
        cost_estimate=cost(1, 1),
    )(me, valid, outer, state, total, part, before, near_stat, qkv_weight, out_weight, taps)


def norm_kernel(
    rows, size, pos_ref, valid_ref, stat_ref, gain_ref, bias_ref, near_ref, far0_ref, far1_ref,
    out_ref, mul_ref, add_ref, mix_ref,
):
    step = pl.program_id(0)
    frames = out_ref.shape[0]
    m = frames * rows
    channels = out_ref.shape[3]
    me = pos_ref[0]
    odd = jnp.bitwise_and(me, 1)

    @pl.when(step == 0)
    def _():
        stat = stat_ref[...]
        tile = lax.broadcasted_iota(jnp.int32, (stat.shape[0], channels), 0)
        counts = jnp.zeros(tile.shape, F32)
        for i in range(stat.shape[0]):
            counts = jnp.where(tile == i, (valid_ref[i] * (2 * rows)).astype(F32), counts)
        mix = jnp.where(same_block((channels, channels), size), 1.0, 0.0)
        all_count = jnp.sum(counts, axis=0, keepdims=True) * (2 * size)

        def grouped(row):
            wide = jnp.broadcast_to(row, (8, channels))
            return dot(wide, mix, precision=lax.Precision.HIGHEST)[0:1]

        sums = stat[:, 0, :] + stat[:, 2, :]
        mean = grouped(jnp.sum(sums, axis=0, keepdims=True)) / all_count
        gap0 = stat[:, 0, :] / counts - mean
        gap1 = stat[:, 2, :] / counts - mean
        spread = stat[:, 1, :] + stat[:, 3, :] + (gap0 * gap0 + gap1 * gap1) * counts
        var = grouped(jnp.sum(spread, axis=0, keepdims=True)) / all_count
        scale = gain_ref[...] * lax.rsqrt(var + 1e-5)
        mul_ref[...] = 0.5 * scale
        add_ref[...] = 0.5 * (bias_ref[...] - mean * scale)

    live = valid_rows(step * frames, valid_ref[me], frames, rows)
    mul, add = mul_ref[...], add_ref[...]
    here = pl.ds(pl.multiple_of(step * m, m), m)
    cut = far0_ref.shape[1]
    there = pl.ds(pl.multiple_of(step * m % cut, m), m)
    late = step * m >= cut
    for y in range(2):
        line = 1 - odd if y == 0 else odd
        for b in range(2):
            if y == 0:
                half = near_ref[b, here] * mul + add
            else:
                half = jnp.where(late, far1_ref[b, there], far0_ref[b, there]) * mul + add
            z = jnp.where(live, half + half * jnp.tanh(half), 0.0)
            for c in range(channels // 128):
                mix_ref[y, c, pl.ds(b, m, 2), :] = z[:, 128 * c : 128 * (c + 1)]
        for f in range(frames):
            for c in range(channels // 128):
                out_ref[f, line, :, 128 * c : 128 * (c + 1)] = mix_ref[
                    y, c, 2 * rows * f : 2 * rows * (f + 1), :
                ].astype(BF)


def norm(rows, me, valid, stat, gain, bias, near_plane, *far_planes):
    count, channels = near_plane.shape[1:]
    n = valid.shape[0]
    frames = 4
    m = frames * rows
    whole = lambda *shape: pl.BlockSpec(shape, lambda i, *_: (0,) * len(shape))
    return pl.pallas_call(
        functools.partial(norm_kernel, rows, channels // NORM_GROUPS),
        grid_spec=pltpu.PrefetchScalarGridSpec(
            num_scalar_prefetch=2,
            grid=(n // frames,),
            in_specs=[
                whole(*stat.shape),
                whole(1, channels),
                whole(1, channels),
                INSIDE,
                INSIDE,
                INSIDE,
            ],
            out_specs=pl.BlockSpec((frames, 2, 2 * rows, channels), lambda i, *_: (i, 0, 0, 0)),
            scratch_shapes=[
                pltpu.VMEM((1, channels), F32),
                pltpu.VMEM((1, channels), F32),
                pltpu.VMEM((2, channels // 128, 2 * m, 128), F32),
            ],
        ),
        out_shape=jax.ShapeDtypeStruct((n, 2, 2 * rows, channels), BF),
        compiler_params=params(24),
        cost_estimate=cost(32 * count * channels, 24 * count * channels, 4 * count * channels),
    )(me, valid, stat, gain.reshape(1, channels), bias.reshape(1, channels), near_plane, *far_planes)


def local(
    tokens,
    qkv_weight,
    out_weight,
    conv_weight,
    norm_gain,
    norm_bias,
    group_map,
    token_order,
    valid_frames,
):
    tiles = lax.axis_size("tm")
    rank = lax.axis_index("tm")
    count, width = tokens.shape
    rows = count // tiles
    channels = conv_weight.shape[3]
    head = width // HEADS
    me = rank.reshape(1).astype(jnp.int32)

    def swap(x, pairs):
        return lax.ppermute(x, "tm", pairs)

    qkv_weight, out_weight, taps = (
        pltpu.with_memory_space_constraint(w, pltpu.HBM)
        for w in (qkv_weight, out_weight, conv_weight.reshape(-1, channels))
    )
    raster = permute(token_order, tokens)
    tile = lax.all_to_all(
        raster.reshape(tiles, rows, width), "tm", split_axis=0, concat_axis=0, tiled=True
    ).reshape(count, width)
    buf = run_state(tokens, qkv_weight, head)

    def swap_by(x, k):
        return swap(x, [(i, i ^ k) for i in range(tiles)])

    k, gate = 2, None
    while k < tiles:
        ks = [k] if k == 2 or 2 * k >= tiles else [k, 2 * k, 3 * k]
        got = [swap_by(buf, j) for j in ks]
        gate = got[0]
        buf = jnp.concatenate([buf] + got, axis=0)
        k *= 2 if len(ks) == 1 else 4
    pieces = [buf, swap_by(buf, 1)]
    tile, _ = lax.optimization_barrier((tile, gate))
    inner = swap_by(tile, 1)
    ends = [(i, i + 1) for i in range(1, tiles - 1, 2)]
    ends = ends + [(j, i) for i, j in ends]
    cut = count // 2
    outer = [swap(tile[:cut], ends), swap(tile[cut:], ends)]
    near_plane, part, state, total, near_stat = near(
        rows, me, group_map, valid_frames, pieces, tile, inner, qkv_weight, out_weight, taps, head
    )
    stat, planes = jnp.zeros((8, channels), F32), []
    for i, piece in enumerate(outer):
        plane, stat = far(
            rows, i * tiles // 2, me, valid_frames, piece, state, total, part, stat, near_stat,
            qkv_weight, out_weight, taps,
        )
        planes.append(plane)
    stat = lax.all_to_all(stat, "tm", split_axis=0, concat_axis=0, tiled=True)
    return norm(rows, me, valid_frames, stat, norm_gain, norm_bias, near_plane, *planes)


def solution(mesh):
    in_specs = (P(("clip", "tm"), None), P(), P(), P(), P(), P(), P("clip"), P("clip"), P("clip"))
    out_specs = P("clip", "tm", None, None)
    return jax.shard_map(local, mesh=mesh, in_specs=in_specs, out_specs=out_specs, check_vma=False)
```

```python
import functools

import jax
import jax.numpy as jnp
from jax import lax
from jax.experimental import pallas as pl
from jax.experimental.pallas import tpu as pltpu
from jax.sharding import PartitionSpec as P

HEADS = 16
NORM_GROUPS = 32
BF = jnp.bfloat16
F32 = jnp.float32
MIB = 1024 * 1024
VMEM = 60
HBM = pl.BlockSpec(memory_space=pltpu.HBM)
ANY = pl.BlockSpec(memory_space=pl.ANY)
INSIDE = pl.BlockSpec(memory_space=pltpu.VMEM)


def dot(a, b, **kw):
    return jnp.dot(a, b, preferred_element_type=F32, **kw)


def params(mib, dims=1):
    return pltpu.CompilerParams(
        vmem_limit_bytes=mib * MIB, dimension_semantics=("arbitrary",) * dims
    )


def cost(flops, nbytes, trans=0):
    return pl.CostEstimate(flops=int(flops), bytes_accessed=int(nbytes), transcendentals=int(trans))


def same_block(shape, size):
    rows = lax.broadcasted_iota(jnp.int32, shape, 0) // size
    cols = lax.broadcasted_iota(jnp.int32, shape, 1) // size
    return rows == cols


def permute_kernel(order_any, tok_any, out_any, order_ref, tok_ref, pick_ref, out_ref, sems):
    count, width = tok_ref.shape
    parts = sems.shape[0] - 2
    rows = count // parts
    loads = [
        pltpu.make_async_copy(order_any, order_ref, sems.at[0]),
        pltpu.make_async_copy(tok_any, tok_ref, sems.at[1]),
    ]
    for copy in loads:
        copy.start()
    loads[0].wait()
    place = lax.broadcasted_iota(jnp.int32, (count, count), 0)
    pick_ref[...] = jnp.where(place == order_ref[...], 1.0, 0.0).astype(BF)
    loads[1].wait()
    stores = []
    for i in range(parts):
        cut = pl.ds(i * rows, rows)
        out_ref[cut] = dot(pick_ref[cut], tok_ref[...]).astype(BF)
        stores.append(pltpu.make_async_copy(out_ref.at[cut], out_any.at[cut], sems.at[2 + i]))
        stores[-1].start()
    for copy in stores:
        copy.wait()


def permute(order, tokens):
    count, width = tokens.shape
    parts = 4
    return pl.pallas_call(
        permute_kernel,
        in_specs=[HBM, HBM],
        out_specs=HBM,
        out_shape=pltpu.HBM((count, width), BF),
        scratch_shapes=[
            pltpu.VMEM((1, count), jnp.int32),
            pltpu.VMEM((count, width), BF),
            pltpu.VMEM((count, count), BF),
            pltpu.VMEM((count, width), BF),
            pltpu.SemaphoreType.DMA((2 + parts,)),
        ],
        compiler_params=pltpu.CompilerParams(vmem_limit_bytes=60 * MIB),
        cost_estimate=cost(2 * count * count * width, 4 * count * width),
    )(order.reshape(1, count), tokens)


def chunk(src, dst, step, m, sem):
    at = pl.ds(pl.multiple_of(step * m, m), m)
    return pltpu.make_async_copy(src.at[at], dst.at[at], sem.at[step])


def spread_row(src, row, dst, sems):
    deep, channels = dst.shape[0] * 3 // 4, dst.shape[1] // 2
    part = src.at[pl.ds(pl.multiple_of(row * deep, deep), deep), :]
    return [
        pltpu.make_async_copy(part, dst.at[:deep, :channels], sems.at[0]),
        pltpu.make_async_copy(part, dst.at[channels:, channels:], sems.at[1]),
    ]


def clear_spread(dst):
    channels = dst.shape[1] // 2
    gap = jnp.zeros((channels, channels), BF)
    dst[3 * channels :, :channels] = gap
    dst[:channels, channels:] = gap


def state_kernel(
    head, pos_ref, tok_ref, wk_ref, wv_ref, qkv_hbm, wo_hbm, taps_hbm,
    out_ref, wq_ref, wo_ref, w2_ref, wx_ref,
    acc_ref, sum_ref, sems,
):
    step = pl.program_id(0)
    odd = jnp.bitwise_and(pos_ref[0], 1)
    channels = taps_hbm.shape[1]
    row = 3 * channels
    first_half = taps_hbm.at[pl.ds(pl.multiple_of(odd * row, row), 2 * row), :]
    second_half = taps_hbm.at[pl.ds(pl.multiple_of((1 - odd) * row, row), 2 * row), :]
    staged = [
        pltpu.make_async_copy(qkv_hbm.at[:, pl.ds(0, wq_ref.shape[1])], wq_ref, sems.at[0]),
        pltpu.make_async_copy(wo_hbm, wo_ref, sems.at[1]),
        pltpu.make_async_copy(first_half, w2_ref.at[:, :channels], sems.at[2]),
        pltpu.make_async_copy(second_half, w2_ref.at[:, channels:], sems.at[3]),
    ]
    staged += spread_row(taps_hbm, 2 * odd, wx_ref, sems.at[pl.ds(4, 2)])
    width = tok_ref.shape[1]
    block = acc_ref.shape[1]

    @pl.when(step == 0)
    def _():
        acc_ref[...] = jnp.zeros_like(acc_ref)
        sum_ref[...] = jnp.zeros_like(sum_ref)
        for copy in staged:
            copy.start()
        clear_spread(wx_ref)

    tok = tok_ref[...]
    keys = jnp.maximum(dot(tok, wk_ref[...]), 0.0)
    keys_b = keys.astype(BF)
    vals_b = dot(tok, wv_ref[...]).astype(BF)
    sum_ref[0:1, :] += jnp.sum(keys_b.astype(F32), axis=0, keepdims=True)
    for i in range(width // block):
        cut = slice(i * block, (i + 1) * block)
        acc_ref[i] += lax.dot_general(
            keys_b[:, cut], vals_b[:, cut], (((0,), (0,)), ((), ())), preferred_element_type=F32
        )

    @pl.when(step == pl.num_programs(0) - 1)
    def _():
        own = same_block((block, block), head)
        parts = []
        for i in range(width // block):
            full = jnp.where(own, acc_ref[i], 0.0)
            small = full[:head]
            for h in range(1, block // head):
                small = small + full[h * head : (h + 1) * head]
            parts.append(small)
        state = jnp.concatenate(parts, axis=1)
        total = sum_ref[0:1, :]
        high = total.astype(BF).astype(F32)
        low = total - high
        lines = [row[:, 128 * i : 128 * (i + 1)] for row in (high, low) for i in range(width // 128)]
        rows = out_ref.shape[1]
        lines.append(jnp.zeros((rows - len(lines), 128), F32))
        cuts = [state[i : i + rows] for i in range(0, head, rows)]
        for copy in staged:
            copy.wait()
        out_ref[0] = jnp.concatenate(cuts + [jnp.concatenate(lines, axis=0)], axis=1).astype(BF)


def unpack(packed, head, width):
    rows = packed.shape[0]
    cuts = head // rows
    state = jnp.concatenate([packed[:, i * width : (i + 1) * width] for i in range(cuts)], axis=0)
    tail = packed[:, cuts * width :]
    lines = width // 128
    both = tail[:lines] + tail[lines : 2 * lines]
    return state, jnp.concatenate([both[i : i + 1] for i in range(lines)], axis=1)


def run_state(me, tokens, qkv_weight, out_weight, taps, head):
    count, width = tokens.shape
    steps, block = 4, 256
    rows = 16
    packed = head // rows * width + 128
    channels = taps.shape[1]
    return pl.pallas_call(
        functools.partial(state_kernel, head),
        grid=(steps,),
        in_specs=[
            pl.BlockSpec(memory_space=pltpu.SMEM),
            pl.BlockSpec((count // steps, width), lambda i: (i, 0)),
            pl.BlockSpec((width, width), lambda i: (0, 1)),
            pl.BlockSpec((width, width), lambda i: (0, 2)),
            HBM,
            HBM,
            HBM,
        ],
        out_specs=[pl.BlockSpec((1, rows, packed), lambda i: (0, 0, 0))] + [INSIDE] * 4,
        out_shape=[
            jax.ShapeDtypeStruct((1, rows, packed), BF),
            pltpu.VMEM((width, width), BF),
            pltpu.VMEM(out_weight.shape, BF),
            pltpu.VMEM((6 * channels, 2 * channels), BF),
            pltpu.VMEM((4 * channels, 2 * channels), BF),
        ],
        scratch_shapes=[
            pltpu.VMEM((width // block, block, block), F32),
            pltpu.VMEM((8, width), F32),
            pltpu.SemaphoreType.DMA((6,)),
        ],
        compiler_params=params(16),
        cost_estimate=cost(4 * count * width * width, 8 * count * width),
    )(me, tokens, qkv_weight, qkv_weight, qkv_weight, out_weight, taps)


def queries(tok, wq):
    return jnp.maximum(dot(tok, wq).astype(BF).astype(F32), 0.0)


def attend(qf, state, total, own, ones):
    block = own.shape[0]
    head, width = state.shape
    qb = qf.astype(BF)
    den_in = (qf * total).astype(BF)
    outs = []
    for i in range(width // block):
        cut = slice(i * block, (i + 1) * block)
        wide = jnp.concatenate([state[:, cut]] * (block // head), axis=0)
        wide = jnp.where(own, wide, jnp.zeros_like(wide))
        numer = dot(qb[:, cut], wide)
        denom = dot(den_in[:, cut], ones) + 1.0
        outs.append(numer / denom)
    return jnp.concatenate(outs, axis=1)


def valid_rows(first, limit, frames, rows):
    frame = lax.broadcasted_iota(jnp.int32, (frames * rows, 1), 0) // rows + first
    return frame < limit


def store_taps(x_ref, at, line, rows):
    m, channels = line.shape[0], line.shape[1] // 2
    column = lax.broadcasted_iota(jnp.int32, (m, 1), 0) % rows
    even_px, odd_px = line[:, :channels], line[:, channels:]
    left = jnp.where(column == 0, 0.0, pltpu.roll(odd_px, 1, 0))
    right = jnp.where(column == rows - 1, 0.0, pltpu.roll(even_px, m - 1, 0))
    for b, taps in enumerate(((left, even_px, odd_px), (even_px, odd_px, right))):
        for d, tap in enumerate(taps):
            cut = slice(at + d * channels, at + (d + 1) * channels)
            x_ref[b * m : (b + 1) * m, cut] = tap.astype(BF)


def line_taps(line, rows):
    m, channels = line.shape[0], line.shape[1] // 2
    column = lax.broadcasted_iota(jnp.int32, (m, 1), 0) % rows
    even_px, odd_px = line[:, :channels], line[:, channels:]
    left = jnp.where(column == 0, 0.0, pltpu.roll(odd_px, 1, 0))
    right = jnp.where(column == rows - 1, 0.0, pltpu.roll(even_px, m - 1, 0))
    return jnp.concatenate([left.astype(BF), line.astype(BF), right.astype(BF)], axis=1)


def gather_stats(run_ref, res, live, limit, first, frames, rows):
    part = jnp.sum(res, axis=0, keepdims=True)
    count = (jnp.clip(limit - first, 0, frames) * (2 * rows)).astype(F32)
    mean = part / jnp.maximum(count, 1.0)
    dev = jnp.where(live, res - mean, 0.0)
    spread = jnp.sum(dev * dev, axis=0, keepdims=True)
    had = (jnp.clip(limit, 0, first) * (2 * rows)).astype(F32)
    run_sum = run_ref[0:1, :]
    gap = mean - run_sum / jnp.maximum(had, 1.0)
    weight = had * count / jnp.maximum(had + count, 1.0)
    run_ref[1:2, :] += spread + gap * gap * weight
    run_ref[0:1, :] = run_sum + part


def near_kernel(
    rows, parts, frames, pos_ref, group_ref, valid_ref, *refs
):
    pieces, refs = refs[: 2 * parts], refs[2 * parts :]
    own_any, inner_any, wq_ref, wo_ref, w2_ref, taps_hbm, *refs = refs
    near_ref, part_ref, state_ref, total_ref, stat_ref, *refs = refs
    acc_ref, pend_ref, att_ref, x_ref, w1_ref, own_ref, inner_ref, buf_ref, *refs = refs
    own_sem, inner_sem, piece_sem, sems = refs
    late = spread_row(taps_hbm, 2 - 2 * jnp.bitwise_and(pos_ref[0], 1), w1_ref, sems)
    step = pl.program_id(0)
    count, width = own_ref.shape
    m = frames * rows
    steps = count // m
    me = pos_ref[0]
    odd = jnp.bitwise_and(me, 1)
    head = state_ref.shape[1]
    channels = near_ref.shape[2]
    size = pieces[0].shape[0]
    fetch = [
        pltpu.make_async_copy(
            pieces[i], buf_ref.at[i // parts, pl.ds(i % parts * size, size)], piece_sem.at[i]
        )
        for i in range(2 * parts)
    ]

    @pl.when(step == 0)
    def _():
        for copy in fetch:
            copy.start()
        for i in range(steps):
            chunk(own_any, own_ref, i, m, own_sem).start()
            chunk(inner_any, inner_ref, i, m, inner_sem).start()
        for copy in late:
            copy.start()
        clear_spread(w1_ref)
        acc_ref[...] = jnp.zeros_like(acc_ref)
        pend_ref[...] = jnp.zeros_like(pend_ref)
        stat_ref[...] = jnp.zeros_like(stat_ref)
        for copy in fetch:
            copy.wait()

    chunk(own_any, own_ref, step, m, own_sem).wait()
    chunk(inner_any, inner_ref, step, m, inner_sem).wait()
    here = pl.ds(pl.multiple_of(step * m, m), m)
    block = 256
    own = same_block((block, block), head)
    ones = jnp.where(own, 1.0, 0.0).astype(BF)
    wq = wq_ref[...]
    q_own = queries(own_ref[here, :], wq)
    q_inner = queries(inner_ref[here, :], wq)
    for i in range(frames):
        frame = step * frames + i
        rel = jnp.bitwise_xor(frame, me)
        piece = buf_ref[jnp.bitwise_and(rel, 1), rel // 2].astype(F32)
        before = group_ref[jnp.maximum(frame - 1, 0)]
        fresh = jnp.where(group_ref[frame] != before, 1.0, 0.0)
        pend = pend_ref[...]
        acc = acc_ref[...] + fresh * pend
        acc_ref[...] = acc
        pend_ref[...] = (1.0 - fresh) * pend + piece
        summed = acc + piece
        state, total = unpack(summed, head, width)
        state = state.astype(BF)
        state_ref[frame] = state
        total_ref[frame] = jnp.broadcast_to(total, (8, width))
        cut = slice(i * rows, (i + 1) * rows)
        both = jnp.concatenate([q_own[cut], q_inner[cut]], axis=0)
        res = attend(both, state, total, own, ones)
        att_ref[0, cut] = res[:rows]
        att_ref[1, cut] = res[rows:]
    first = step * frames
    limit = valid_ref[me]
    keep_own = valid_rows(first, limit, frames, rows)
    keep_inner = valid_rows(first, valid_ref[jnp.bitwise_xor(me, 1)], frames, rows)

    @pl.when(step == 0)
    def _():
        for copy in late:
            copy.wait()

    half, row = 2 * channels, 3 * channels
    mine = jnp.where(keep_own, dot(att_ref[0].astype(BF), wo_ref[...]), 0.0)
    w_close = wo_ref[:, pl.ds(pl.multiple_of(odd * half, half), half)]
    close = jnp.where(keep_inner, dot(att_ref[1].astype(BF), w_close), 0.0)
    store_taps(x_ref, 0, mine[:, : 2 * channels], rows)
    store_taps(x_ref, row, mine[:, 2 * channels :], rows)
    live = jnp.concatenate([keep_own, keep_own], axis=0)
    pair = dot(x_ref[...], w2_ref[...])
    more = dot(line_taps(close, rows), w1_ref[...])
    more = jnp.concatenate([more[:, :channels], more[:, channels:]], axis=0)
    res = jnp.where(live, pair[:, :channels] + more, 0.0)
    near_ref[0, here] = res[:m]
    near_ref[1, here] = res[m:]
    gather_stats(stat_ref, res, live, limit, first, frames, rows)
    part_ref[0, here] = pair[:m, channels:]
    part_ref[1, here] = pair[m:, channels:]


def near(rows, me, group_map, valid, pieces, own, inner, weights, channels, head):
    count, width = own.shape
    frames = 16
    n = count // rows
    m = frames * rows
    deep, packed = pieces[0].shape[1:]
    parts = len(pieces) // 2
    return pl.pallas_call(
        functools.partial(near_kernel, rows, parts, frames),
        grid_spec=pltpu.PrefetchScalarGridSpec(
            num_scalar_prefetch=3,
            grid=(n // frames,),
            in_specs=[ANY] * (2 * parts + 2) + [INSIDE] * 3 + [HBM],
            out_specs=[INSIDE] * 5,
            scratch_shapes=[
                pltpu.VMEM((deep, packed), F32),
                pltpu.VMEM((deep, packed), F32),
                pltpu.VMEM((2, m, width), F32),
                pltpu.VMEM((2 * m, 6 * channels), BF),
                pltpu.VMEM((4 * channels, 2 * channels), BF),
                pltpu.VMEM((count, width), BF),
                pltpu.VMEM((count, width), BF),
                pltpu.VMEM((2, n // 2, deep, packed), BF),
                pltpu.SemaphoreType.DMA((n // frames,)),
                pltpu.SemaphoreType.DMA((n // frames,)),
                pltpu.SemaphoreType.DMA((2 * parts,)),
                pltpu.SemaphoreType.DMA((2,)),
            ],
        ),
        out_shape=[
            pltpu.VMEM((2, count, channels), F32),
            pltpu.VMEM((2, count, channels), F32),
            pltpu.VMEM((n, head, width), BF),
            pltpu.VMEM((n, 8, width), F32),
            pltpu.VMEM((8, channels), F32),
        ],
        compiler_params=params(32),
        cost_estimate=cost(1, 1),
    )(me, group_map, valid, *pieces, own, inner, *weights)


def far_kernel(
    rows, first, last, pos_ref, valid_ref,
    outer_any, state_ref, total_ref, part_ref, before_ref, near_stat_ref, wq_ref, wo_ref, wx_ref,
    far_ref, stat_ref,
    att_ref, run_ref, outer_ref, sem,
):
    m, width = outer_ref.shape
    channels = far_ref.shape[2]
    frames = m // rows
    me = pos_ref[0]
    odd = jnp.bitwise_and(me, 1)
    head = state_ref.shape[1]
    half = 2 * channels
    half_at = pl.ds(pl.multiple_of((1 - odd) * half, half), half)
    copy = pltpu.make_async_copy(outer_any, outer_ref, sem)
    copy.start()
    run_ref[...] = before_ref[...]
    block = 256
    own = same_block((block, block), head)
    ones = jnp.where(own, 1.0, 0.0).astype(BF)
    copy.wait()
    qf = queries(outer_ref[...], wq_ref[...])
    for i in range(frames):
        cut = slice(i * rows, (i + 1) * rows)
        frame = first + i
        att_ref[cut] = attend(qf[cut], state_ref[frame], total_ref[frame][0:1], own, ones)
    outer_at = jnp.clip(me + 2 * odd - 1, 0, valid_ref.shape[0] - 1)
    keep = valid_rows(first, valid_ref[outer_at], frames, rows)
    line = jnp.where(keep, dot(att_ref[...].astype(BF), wo_ref[:, half_at]), 0.0)
    more = dot(line_taps(line, rows), wx_ref[...])
    more = jnp.concatenate([more[:, :channels], more[:, channels:]], axis=0)
    limit = valid_ref[me]
    live = valid_rows(first, limit, frames, rows)
    live = jnp.concatenate([live, live], axis=0)
    here = pl.ds(first * rows, m)
    part = jnp.concatenate([part_ref[0, here], part_ref[1, here]], axis=0)
    res = jnp.where(live, part + more, 0.0)
    far_ref[0] = res[:m]
    far_ref[1] = res[m:]
    gather_stats(run_ref, res, live, limit, first, frames, rows)
    if last:
        both = jnp.concatenate([near_stat_ref[0:2], run_ref[0:2], run_ref[4:8]], axis=0)
        stat_ref[...] = jnp.broadcast_to(both[None], stat_ref.shape)
    else:
        stat_ref[...] = run_ref[...]


def far(rows, first, me, valid, outer, state, total, part, before, near_stat, weights):
    m, width = outer.shape
    channels = part.shape[2]
    n = state.shape[0]
    last = first + m // rows == n
    smem = pl.BlockSpec(memory_space=pltpu.SMEM)
    stat = jax.ShapeDtypeStruct((n, 8, channels), F32) if last else pltpu.VMEM((8, channels), F32)
    return pl.pallas_call(
        functools.partial(far_kernel, rows, first, last),
        in_specs=[smem, smem, ANY] + [INSIDE] * 8,
        out_specs=[INSIDE, INSIDE],
        scratch_shapes=[
            pltpu.VMEM((m, width), F32),
            pltpu.VMEM((8, channels), F32),
            pltpu.VMEM((m, width), BF),
            pltpu.SemaphoreType.DMA,
        ],
        out_shape=[pltpu.VMEM((2, m, channels), F32), stat],
        compiler_params=pltpu.CompilerParams(vmem_limit_bytes=16 * MIB),
        cost_estimate=cost(1, 1),
    )(me, valid, outer, state, total, part, before, near_stat, *weights)


def norm_kernel(
    rows, size, pos_ref, valid_ref, stat_ref, gain_ref, bias_ref, near_ref, far0_ref, far1_ref,
    out_ref, mul_ref, add_ref, mix_ref,
):
    step = pl.program_id(0)
    frames = out_ref.shape[0]
    m = frames * rows
    channels = out_ref.shape[3]
    me = pos_ref[0]
    odd = jnp.bitwise_and(me, 1)

    @pl.when(step == 0)
    def _():
        stat = stat_ref[...]
        tile = lax.broadcasted_iota(jnp.int32, (stat.shape[0], channels), 0)
        counts = jnp.zeros(tile.shape, F32)
        for i in range(stat.shape[0]):
            counts = jnp.where(tile == i, (valid_ref[i] * (2 * rows)).astype(F32), counts)
        mix = jnp.where(same_block((channels, channels), size), 1.0, 0.0)
        all_count = jnp.sum(counts, axis=0, keepdims=True) * (2 * size)

        def grouped(row):
            wide = jnp.broadcast_to(row, (8, channels))
            return dot(wide, mix, precision=lax.Precision.HIGHEST)[0:1]

        sums = stat[:, 0, :] + stat[:, 2, :]
        mean = grouped(jnp.sum(sums, axis=0, keepdims=True)) / all_count
        gap0 = stat[:, 0, :] / counts - mean
        gap1 = stat[:, 2, :] / counts - mean
        spread = stat[:, 1, :] + stat[:, 3, :] + (gap0 * gap0 + gap1 * gap1) * counts
        var = grouped(jnp.sum(spread, axis=0, keepdims=True)) / all_count
        scale = gain_ref[...] * lax.rsqrt(var + 1e-5)
        mul_ref[...] = 0.5 * scale
        add_ref[...] = 0.5 * (bias_ref[...] - mean * scale)

    live = valid_rows(step * frames, valid_ref[me], frames, rows)
    mul, add = mul_ref[...], add_ref[...]
    here = pl.ds(pl.multiple_of(step * m, m), m)
    cut = far0_ref.shape[1]
    there = pl.ds(pl.multiple_of(step * m % cut, m), m)
    late = step * m >= cut
    for y in range(2):
        line = 1 - odd if y == 0 else odd
        for b in range(2):
            if y == 0:
                half = near_ref[b, here] * mul + add
            else:
                half = jnp.where(late, far1_ref[b, there], far0_ref[b, there]) * mul + add
            z = jnp.where(live, half + half * jnp.tanh(half), 0.0)
            for c in range(channels // 128):
                mix_ref[y, c, pl.ds(b, m, 2), :] = z[:, 128 * c : 128 * (c + 1)]
        for f in range(frames):
            for c in range(channels // 128):
                out_ref[f, line, :, 128 * c : 128 * (c + 1)] = mix_ref[
                    y, c, 2 * rows * f : 2 * rows * (f + 1), :
                ].astype(BF)


def norm(rows, me, valid, stat, gain, bias, near_plane, *far_planes):
    count, channels = near_plane.shape[1:]
    n = valid.shape[0]
    frames = 4
    m = frames * rows
    whole = lambda *shape: pl.BlockSpec(shape, lambda i, *_: (0,) * len(shape))
    return pl.pallas_call(
        functools.partial(norm_kernel, rows, channels // NORM_GROUPS),
        grid_spec=pltpu.PrefetchScalarGridSpec(
            num_scalar_prefetch=2,
            grid=(n // frames,),
            in_specs=[
                whole(*stat.shape),
                whole(1, channels),
                whole(1, channels),
                INSIDE,
                INSIDE,
                INSIDE,
            ],
            out_specs=pl.BlockSpec((frames, 2, 2 * rows, channels), lambda i, *_: (i, 0, 0, 0)),
            scratch_shapes=[
                pltpu.VMEM((1, channels), F32),
                pltpu.VMEM((1, channels), F32),
                pltpu.VMEM((2, channels // 128, 2 * m, 128), F32),
            ],
        ),
        out_shape=jax.ShapeDtypeStruct((n, 2, 2 * rows, channels), BF),
        compiler_params=params(24),
        cost_estimate=cost(32 * count * channels, 24 * count * channels, 4 * count * channels),
    )(me, valid, stat, gain.reshape(1, channels), bias.reshape(1, channels), near_plane, *far_planes)


def local(
    tokens,
    qkv_weight,
    out_weight,
    conv_weight,
    norm_gain,
    norm_bias,
    group_map,
    token_order,
    valid_frames,
):
    tiles = lax.axis_size("tm")
    rank = lax.axis_index("tm")
    count, width = tokens.shape
    rows = count // tiles
    channels = conv_weight.shape[3]
    head = width // HEADS
    me = rank.reshape(1).astype(jnp.int32)

    def swap(x, pairs):
        return lax.ppermute(x, "tm", pairs)

    qkv_weight, out_weight, taps = (
        pltpu.with_memory_space_constraint(w, pltpu.HBM)
        for w in (qkv_weight, out_weight, conv_weight.reshape(-1, channels))
    )
    raster = permute(token_order, tokens)
    tile = lax.all_to_all(
        raster.reshape(tiles, rows, width), "tm", split_axis=0, concat_axis=0, tiled=True
    ).reshape(count, width)
    buf, wq, wo, w2, wx = run_state(me, tokens, qkv_weight, out_weight, taps, head)

    def swap_by(x, k):
        return swap(x, [(i, i ^ k) for i in range(tiles)])

    k, gate = 2, None
    while k < tiles:
        ks = [k] if k == 2 or 2 * k >= tiles else [k, 2 * k, 3 * k]
        got = [swap_by(buf, j) for j in ks]
        gate = got[0]
        buf = jnp.concatenate([buf] + got, axis=0)
        k *= 2 if len(ks) == 1 else 4
    pieces = [buf, swap_by(buf, 1)]
    tile, _ = lax.optimization_barrier((tile, gate))
    inner = swap_by(tile, 1)
    ends = [(i, i + 1) for i in range(1, tiles - 1, 2)]
    ends = ends + [(j, i) for i, j in ends]
    cut = count // 2
    outer = [swap(tile[:cut], ends), swap(tile[cut:], ends)]
    near_plane, part, state, total, near_stat = near(
        rows, me, group_map, valid_frames, pieces, tile, inner, (wq, wo, w2, taps),
        channels, head,
    )
    stat, planes = jnp.zeros((8, channels), F32), []
    for i, piece in enumerate(outer):
        plane, stat = far(
            rows, i * tiles // 2, me, valid_frames, piece, state, total, part, stat, near_stat,
            (wq, wo, wx),
        )
        planes.append(plane)
    stat = lax.all_to_all(stat, "tm", split_axis=0, concat_axis=0, tiled=True)
    return norm(rows, me, valid_frames, stat, norm_gain, norm_bias, near_plane, *planes)


def solution(mesh):
    in_specs = (P(("clip", "tm"), None), P(), P(), P(), P(), P(), P("clip"), P("clip"), P("clip"))
    out_specs = P("clip", "tm", None, None)
    return jax.shard_map(local, mesh=mesh, in_specs=in_specs, out_specs=out_specs, check_vma=False)
```

```python
import functools

import jax
import jax.numpy as jnp
from jax import lax
from jax.experimental import pallas as pl
from jax.experimental.pallas import tpu as pltpu
from jax.sharding import PartitionSpec as P

HEADS = 16
NORM_GROUPS = 32
BF = jnp.bfloat16
F32 = jnp.float32
MIB = 1024 * 1024
VMEM = 60
HBM = pl.BlockSpec(memory_space=pltpu.HBM)
ANY = pl.BlockSpec(memory_space=pl.ANY)
INSIDE = pl.BlockSpec(memory_space=pltpu.VMEM)


def dot(a, b, **kw):
    return jnp.dot(a, b, preferred_element_type=F32, **kw)


def params(mib, dims=1):
    return pltpu.CompilerParams(
        vmem_limit_bytes=mib * MIB, dimension_semantics=("arbitrary",) * dims
    )


def cost(flops, nbytes, trans=0):
    return pl.CostEstimate(flops=int(flops), bytes_accessed=int(nbytes), transcendentals=int(trans))


def same_block(shape, size):
    rows = lax.broadcasted_iota(jnp.int32, shape, 0) // size
    cols = lax.broadcasted_iota(jnp.int32, shape, 1) // size
    return rows == cols


def permute_kernel(order_any, tok_any, out_any, order_ref, tok_ref, pick_ref, out_ref, sems):
    count, width = tok_ref.shape
    parts = sems.shape[0] - 2
    rows = count // parts
    loads = [
        pltpu.make_async_copy(order_any, order_ref, sems.at[0]),
        pltpu.make_async_copy(tok_any, tok_ref, sems.at[1]),
    ]
    for copy in loads:
        copy.start()
    loads[0].wait()
    place = lax.broadcasted_iota(jnp.int32, (count, count), 0)
    pick_ref[...] = jnp.where(place == order_ref[...], 1.0, 0.0).astype(BF)
    loads[1].wait()
    stores = []
    for i in range(parts):
        cut = pl.ds(i * rows, rows)
        out_ref[cut] = dot(pick_ref[cut], tok_ref[...]).astype(BF)
        stores.append(pltpu.make_async_copy(out_ref.at[cut], out_any.at[cut], sems.at[2 + i]))
        stores[-1].start()
    for copy in stores:
        copy.wait()


def permute(order, tokens):
    count, width = tokens.shape
    parts = 4
    return pl.pallas_call(
        permute_kernel,
        in_specs=[HBM, HBM],
        out_specs=HBM,
        out_shape=pltpu.HBM((count, width), BF),
        scratch_shapes=[
            pltpu.VMEM((1, count), jnp.int32),
            pltpu.VMEM((count, width), BF),
            pltpu.VMEM((count, count), BF),
            pltpu.VMEM((count, width), BF),
            pltpu.SemaphoreType.DMA((2 + parts,)),
        ],
        compiler_params=pltpu.CompilerParams(vmem_limit_bytes=60 * MIB),
        cost_estimate=cost(2 * count * count * width, 4 * count * width),
    )(order.reshape(1, count), tokens)


def chunk(src, dst, step, m, sem):
    at = pl.ds(pl.multiple_of(step * m, m), m)
    return pltpu.make_async_copy(src.at[at], dst.at[at], sem.at[step])


def spread_row(src, row, dst, sems):
    deep, channels = dst.shape[0] * 3 // 4, dst.shape[1] // 2
    part = src.at[pl.ds(pl.multiple_of(row * deep, deep), deep), :]
    return [
        pltpu.make_async_copy(part, dst.at[:deep, :channels], sems.at[0]),
        pltpu.make_async_copy(part, dst.at[channels:, channels:], sems.at[1]),
    ]


def clear_spread(dst):
    channels = dst.shape[1] // 2
    gap = jnp.zeros((channels, channels), BF)
    dst[3 * channels :, :channels] = gap
    dst[:channels, channels:] = gap


def state_kernel(
    head, pos_ref, tok_ref, wk_ref, wv_ref, qkv_hbm, wo_hbm, taps_hbm,
    out_ref, wq_ref, wo_ref, w2_ref, wx_ref,
    acc_ref, sum_ref, sems,
):
    step = pl.program_id(0)
    odd = jnp.bitwise_and(pos_ref[0], 1)
    channels = taps_hbm.shape[1]
    row = 3 * channels
    first_half = taps_hbm.at[pl.ds(pl.multiple_of(odd * row, row), 2 * row), :]
    second_half = taps_hbm.at[pl.ds(pl.multiple_of((1 - odd) * row, row), 2 * row), :]
    staged = [
        pltpu.make_async_copy(qkv_hbm.at[:, pl.ds(0, wq_ref.shape[1])], wq_ref, sems.at[0]),
        pltpu.make_async_copy(wo_hbm, wo_ref, sems.at[1]),
        pltpu.make_async_copy(first_half, w2_ref.at[:, :channels], sems.at[2]),
        pltpu.make_async_copy(second_half, w2_ref.at[:, channels:], sems.at[3]),
    ]
    staged += spread_row(taps_hbm, 2 * odd, wx_ref, sems.at[pl.ds(4, 2)])
    width = tok_ref.shape[1]
    block = acc_ref.shape[1]

    @pl.when(step == 0)
    def _():
        acc_ref[...] = jnp.zeros_like(acc_ref)
        sum_ref[...] = jnp.zeros_like(sum_ref)
        for copy in staged:
            copy.start()
        clear_spread(wx_ref)

    tok = tok_ref[...]
    keys = jnp.maximum(dot(tok, wk_ref[...]), 0.0)
    keys_b = keys.astype(BF)
    vals_b = dot(tok, wv_ref[...]).astype(BF)
    sum_ref[0:1, :] += jnp.sum(keys_b.astype(F32), axis=0, keepdims=True)
    for i in range(width // block):
        cut = slice(i * block, (i + 1) * block)
        acc_ref[i] += lax.dot_general(
            keys_b[:, cut], vals_b[:, cut], (((0,), (0,)), ((), ())), preferred_element_type=F32
        )

    @pl.when(step == pl.num_programs(0) - 1)
    def _():
        own = same_block((block, block), head)
        parts = []
        for i in range(width // block):
            full = jnp.where(own, acc_ref[i], 0.0)
            small = full[:head]
            for h in range(1, block // head):
                small = small + full[h * head : (h + 1) * head]
            parts.append(small)
        state = jnp.concatenate(parts, axis=1)
        total = sum_ref[0:1, :]
        high = total.astype(BF).astype(F32)
        low = total - high
        lines = [row[:, 128 * i : 128 * (i + 1)] for row in (high, low) for i in range(width // 128)]
        rows = out_ref.shape[1]
        lines.append(jnp.zeros((rows - len(lines), 128), F32))
        cuts = [state[i : i + rows] for i in range(0, head, rows)]
        for copy in staged:
            copy.wait()
        out_ref[0] = jnp.concatenate(cuts + [jnp.concatenate(lines, axis=0)], axis=1).astype(BF)


def unpack(packed, head, width):
    rows = packed.shape[0]
    cuts = head // rows
    state = jnp.concatenate([packed[:, i * width : (i + 1) * width] for i in range(cuts)], axis=0)
    tail = packed[:, cuts * width :]
    lines = width // 128
    both = tail[:lines] + tail[lines : 2 * lines]
    return state, jnp.concatenate([both[i : i + 1] for i in range(lines)], axis=1)


def run_state(me, tokens, qkv_weight, out_weight, taps, head):
    count, width = tokens.shape
    steps, block = 4, 256
    rows = 16
    packed = head // rows * width + 128
    channels = taps.shape[1]
    return pl.pallas_call(
        functools.partial(state_kernel, head),
        grid=(steps,),
        in_specs=[
            pl.BlockSpec(memory_space=pltpu.SMEM),
            pl.BlockSpec((count // steps, width), lambda i: (i, 0)),
            pl.BlockSpec((width, width), lambda i: (0, 1)),
            pl.BlockSpec((width, width), lambda i: (0, 2)),
            HBM,
            HBM,
            HBM,
        ],
        out_specs=[pl.BlockSpec((1, rows, packed), lambda i: (0, 0, 0))] + [INSIDE] * 4,
        out_shape=[
            jax.ShapeDtypeStruct((1, rows, packed), BF),
            pltpu.VMEM((width, width), BF),
            pltpu.VMEM(out_weight.shape, BF),
            pltpu.VMEM((6 * channels, 2 * channels), BF),
            pltpu.VMEM((4 * channels, 2 * channels), BF),
        ],
        scratch_shapes=[
            pltpu.VMEM((width // block, block, block), F32),
            pltpu.VMEM((8, width), F32),
            pltpu.SemaphoreType.DMA((6,)),
        ],
        compiler_params=params(16),
        cost_estimate=cost(4 * count * width * width, 8 * count * width),
    )(me, tokens, qkv_weight, qkv_weight, qkv_weight, out_weight, taps)


def queries(tok, wq):
    return jnp.maximum(dot(tok, wq).astype(BF).astype(F32), 0.0)


def attend(qf, state, total, own, ones):
    block = own.shape[0]
    head, width = state.shape
    qb = qf.astype(BF)
    den_in = (qf * total).astype(BF)
    outs = []
    for i in range(width // block):
        cut = slice(i * block, (i + 1) * block)
        wide = jnp.concatenate([state[:, cut]] * (block // head), axis=0)
        wide = jnp.where(own, wide, jnp.zeros_like(wide))
        numer = dot(qb[:, cut], wide)
        denom = dot(den_in[:, cut], ones) + 1.0
        outs.append(numer / denom)
    return jnp.concatenate(outs, axis=1)


def valid_rows(first, limit, frames, rows):
    frame = lax.broadcasted_iota(jnp.int32, (frames * rows, 1), 0) // rows + first
    return frame < limit


def store_taps(x_ref, at, line, rows):
    m, channels = line.shape[0], line.shape[1] // 2
    column = lax.broadcasted_iota(jnp.int32, (m, 1), 0) % rows
    even_px, odd_px = line[:, :channels], line[:, channels:]
    left = jnp.where(column == 0, 0.0, pltpu.roll(odd_px, 1, 0))
    right = jnp.where(column == rows - 1, 0.0, pltpu.roll(even_px, m - 1, 0))
    for b, taps in enumerate(((left, even_px, odd_px), (even_px, odd_px, right))):
        for d, tap in enumerate(taps):
            cut = slice(at + d * channels, at + (d + 1) * channels)
            x_ref[b * m : (b + 1) * m, cut] = tap.astype(BF)


def line_taps(line, rows):
    m, channels = line.shape[0], line.shape[1] // 2
    column = lax.broadcasted_iota(jnp.int32, (m, 1), 0) % rows
    even_px, odd_px = line[:, :channels], line[:, channels:]
    left = jnp.where(column == 0, 0.0, pltpu.roll(odd_px, 1, 0))
    right = jnp.where(column == rows - 1, 0.0, pltpu.roll(even_px, m - 1, 0))
    return jnp.concatenate([left.astype(BF), line.astype(BF), right.astype(BF)], axis=1)


def gather_stats(run_ref, res, live, limit, first, frames, rows):
    part = jnp.sum(res, axis=0, keepdims=True)
    count = (jnp.clip(limit - first, 0, frames) * (2 * rows)).astype(F32)
    mean = part / jnp.maximum(count, 1.0)
    dev = jnp.where(live, res - mean, 0.0)
    spread = jnp.sum(dev * dev, axis=0, keepdims=True)
    had = (jnp.clip(limit, 0, first) * (2 * rows)).astype(F32)
    run_sum = run_ref[0:1, :]
    gap = mean - run_sum / jnp.maximum(had, 1.0)
    weight = had * count / jnp.maximum(had + count, 1.0)
    run_ref[1:2, :] += spread + gap * gap * weight
    run_ref[0:1, :] = run_sum + part


def near_kernel(
    rows, parts, frames, pos_ref, group_ref, valid_ref, *refs
):
    pieces, refs = refs[: 2 * parts], refs[2 * parts :]
    own_any, inner_any, wq_ref, wo_ref, w2_ref, taps_hbm, *refs = refs
    near_ref, part_ref, state_ref, total_ref, stat_ref, *refs = refs
    acc_ref, pend_ref, att_ref, x_ref, w1_ref, own_ref, inner_ref, buf_ref, *refs = refs
    own_sem, inner_sem, piece_sem, sems = refs
    late = spread_row(taps_hbm, 2 - 2 * jnp.bitwise_and(pos_ref[0], 1), w1_ref, sems)
    step = pl.program_id(0)
    count, width = own_ref.shape
    m = frames * rows
    steps = count // m
    me = pos_ref[0]
    odd = jnp.bitwise_and(me, 1)
    head = state_ref.shape[1]
    channels = near_ref.shape[2]
    size = pieces[0].shape[0]
    fetch = [
        pltpu.make_async_copy(
            pieces[i], buf_ref.at[i // parts, pl.ds(i % parts * size, size)], piece_sem.at[i]
        )
        for i in range(2 * parts)
    ]

    @pl.when(step == 0)
    def _():
        for copy in fetch:
            copy.start()
        for i in range(steps):
            chunk(own_any, own_ref, i, m, own_sem).start()
            chunk(inner_any, inner_ref, i, m, inner_sem).start()
        for copy in late:
            copy.start()
        clear_spread(w1_ref)
        acc_ref[...] = jnp.zeros_like(acc_ref)
        pend_ref[...] = jnp.zeros_like(pend_ref)
        stat_ref[...] = jnp.zeros_like(stat_ref)
        for copy in fetch:
            copy.wait()

    chunk(own_any, own_ref, step, m, own_sem).wait()
    chunk(inner_any, inner_ref, step, m, inner_sem).wait()
    here = pl.ds(pl.multiple_of(step * m, m), m)
    block = 256
    own = same_block((block, block), head)
    ones = jnp.where(own, 1.0, 0.0).astype(BF)
    wq = wq_ref[...]
    q_own = queries(own_ref[here, :], wq)
    q_inner = queries(inner_ref[here, :], wq)
    for i in range(frames):
        frame = step * frames + i
        rel = jnp.bitwise_xor(frame, me)
        piece = buf_ref[jnp.bitwise_and(rel, 1), rel // 2].astype(F32)
        before = group_ref[jnp.maximum(frame - 1, 0)]
        fresh = jnp.where(group_ref[frame] != before, 1.0, 0.0)
        pend = pend_ref[...]
        acc = acc_ref[...] + fresh * pend
        acc_ref[...] = acc
        pend_ref[...] = (1.0 - fresh) * pend + piece
        summed = acc + piece
        state, total = unpack(summed, head, width)
        state = state.astype(BF)
        state_ref[frame] = state
        total_ref[frame] = jnp.broadcast_to(total, (8, width))
        cut = slice(i * rows, (i + 1) * rows)
        both = jnp.concatenate([q_own[cut], q_inner[cut]], axis=0)
        res = attend(both, state, total, own, ones)
        att_ref[0, cut] = res[:rows]
        att_ref[1, cut] = res[rows:]
    first = step * frames
    limit = valid_ref[me]
    keep_own = valid_rows(first, limit, frames, rows)
    keep_inner = valid_rows(first, valid_ref[jnp.bitwise_xor(me, 1)], frames, rows)

    @pl.when(step == 0)
    def _():
        for copy in late:
            copy.wait()

    half, row = 2 * channels, 3 * channels
    mine = jnp.where(keep_own, dot(att_ref[0].astype(BF), wo_ref[...]), 0.0)
    w_close = wo_ref[:, pl.ds(pl.multiple_of(odd * half, half), half)]
    close = jnp.where(keep_inner, dot(att_ref[1].astype(BF), w_close), 0.0)
    store_taps(x_ref, 0, mine[:, : 2 * channels], rows)
    store_taps(x_ref, row, mine[:, 2 * channels :], rows)
    live = jnp.concatenate([keep_own, keep_own], axis=0)
    pair = dot(x_ref[...], w2_ref[...])
    more = dot(line_taps(close, rows), w1_ref[...])
    more = jnp.concatenate([more[:, :channels], more[:, channels:]], axis=0)
    res = jnp.where(live, pair[:, :channels] + more, 0.0)
    near_ref[0, here] = res[:m]
    near_ref[1, here] = res[m:]
    gather_stats(stat_ref, res, live, limit, first, frames, rows)
    part_ref[0, here] = pair[:m, channels:]
    part_ref[1, here] = pair[m:, channels:]


def near(rows, me, group_map, valid, pieces, own, inner, weights, channels, head):
    count, width = own.shape
    frames = 16
    n = count // rows
    m = frames * rows
    deep, packed = pieces[0].shape[1:]
    parts = len(pieces) // 2
    return pl.pallas_call(
        functools.partial(near_kernel, rows, parts, frames),
        grid_spec=pltpu.PrefetchScalarGridSpec(
            num_scalar_prefetch=3,
            grid=(n // frames,),
            in_specs=[ANY] * (2 * parts + 2) + [INSIDE] * 3 + [HBM],
            out_specs=[INSIDE] * 5,
            scratch_shapes=[
                pltpu.VMEM((deep, packed), F32),
                pltpu.VMEM((deep, packed), F32),
                pltpu.VMEM((2, m, width), F32),
                pltpu.VMEM((2 * m, 6 * channels), BF),
                pltpu.VMEM((4 * channels, 2 * channels), BF),
                pltpu.VMEM((count, width), BF),
                pltpu.VMEM((count, width), BF),
                pltpu.VMEM((2, n // 2, deep, packed), BF),
                pltpu.SemaphoreType.DMA((n // frames,)),
                pltpu.SemaphoreType.DMA((n // frames,)),
                pltpu.SemaphoreType.DMA((2 * parts,)),
                pltpu.SemaphoreType.DMA((2,)),
            ],
        ),
        out_shape=[
            pltpu.VMEM((2, count, channels), F32),
            pltpu.VMEM((2, count, channels), F32),
            pltpu.VMEM((n, head, width), BF),
            pltpu.VMEM((n, 8, width), F32),
            pltpu.VMEM((8, channels), F32),
        ],
        compiler_params=params(32),
        cost_estimate=cost(1, 1),
    )(me, group_map, valid, *pieces, own, inner, *weights)


def far_kernel(
    rows, first, last, pos_ref, valid_ref,
    outer_any, state_ref, total_ref, part_ref, before_ref, near_stat_ref, wq_ref, wo_ref, wx_ref,
    far_ref, stat_ref,
    att_ref, run_ref, outer_ref, sem,
):
    m, width = outer_ref.shape
    channels = far_ref.shape[2]
    frames = m // rows
    me = pos_ref[0]
    odd = jnp.bitwise_and(me, 1)
    head = state_ref.shape[1]
    half = 2 * channels
    half_at = pl.ds(pl.multiple_of((1 - odd) * half, half), half)
    copy = pltpu.make_async_copy(outer_any, outer_ref, sem)
    copy.start()
    run_ref[...] = before_ref[...]
    block = 256
    own = same_block((block, block), head)
    ones = jnp.where(own, 1.0, 0.0).astype(BF)
    copy.wait()
    qf = queries(outer_ref[...], wq_ref[...])
    for i in range(frames):
        cut = slice(i * rows, (i + 1) * rows)
        frame = first + i
        att_ref[cut] = attend(qf[cut], state_ref[frame], total_ref[frame][0:1], own, ones)
    outer_at = jnp.clip(me + 2 * odd - 1, 0, valid_ref.shape[0] - 1)
    keep = valid_rows(first, valid_ref[outer_at], frames, rows)
    line = jnp.where(keep, dot(att_ref[...].astype(BF), wo_ref[:, half_at]), 0.0)
    more = dot(line_taps(line, rows), wx_ref[...])
    more = jnp.concatenate([more[:, :channels], more[:, channels:]], axis=0)
    limit = valid_ref[me]
    live = valid_rows(first, limit, frames, rows)
    live = jnp.concatenate([live, live], axis=0)
    here = pl.ds(first * rows, m)
    part = jnp.concatenate([part_ref[0, here], part_ref[1, here]], axis=0)
    res = jnp.where(live, part + more, 0.0)
    far_ref[0] = res[:m]
    far_ref[1] = res[m:]
    gather_stats(run_ref, res, live, limit, first, frames, rows)
    if last:
        both = jnp.concatenate([near_stat_ref[0:2], run_ref[0:2], run_ref[4:8]], axis=0)
        stat_ref[...] = jnp.broadcast_to(both[None], stat_ref.shape)
    else:
        stat_ref[...] = run_ref[...]


def far(rows, first, me, valid, outer, state, total, part, before, near_stat, weights):
    m, width = outer.shape
    channels = part.shape[2]
    n = state.shape[0]
    last = first + m // rows == n
    smem = pl.BlockSpec(memory_space=pltpu.SMEM)
    stat = jax.ShapeDtypeStruct((n, 8, channels), F32) if last else pltpu.VMEM((8, channels), F32)
    return pl.pallas_call(
        functools.partial(far_kernel, rows, first, last),
        in_specs=[smem, smem, ANY] + [INSIDE] * 8,
        out_specs=[INSIDE, INSIDE],
        scratch_shapes=[
            pltpu.VMEM((m, width), F32),
            pltpu.VMEM((8, channels), F32),
            pltpu.VMEM((m, width), BF),
            pltpu.SemaphoreType.DMA,
        ],
        out_shape=[pltpu.VMEM((2, m, channels), F32), stat],
        compiler_params=pltpu.CompilerParams(vmem_limit_bytes=16 * MIB),
        cost_estimate=cost(1, 1),
    )(me, valid, outer, state, total, part, before, near_stat, *weights)


def norm_kernel(
    rows, size, frames, pos_ref, valid_ref, stat_ref, gain_ref, bias_ref, near_ref, far0_ref, far1_ref,
    out_hbm, mix_ref, out_ref, sems,
):
    m = frames * rows
    channels = out_ref.shape[3]
    me = pos_ref[0]
    odd = jnp.bitwise_and(me, 1)

    stat = stat_ref[...]
    tile = lax.broadcasted_iota(jnp.int32, (stat.shape[0], channels), 0)
    counts = jnp.zeros(tile.shape, F32)
    for i in range(stat.shape[0]):
        counts = jnp.where(tile == i, (valid_ref[i] * (2 * rows)).astype(F32), counts)
    mix = jnp.where(same_block((channels, channels), size), 1.0, 0.0)
    all_count = jnp.sum(counts, axis=0, keepdims=True) * (2 * size)

    def grouped(row):
        wide = jnp.broadcast_to(row, (8, channels))
        return dot(wide, mix, precision=lax.Precision.HIGHEST)[0:1]

    sums = stat[:, 0, :] + stat[:, 2, :]
    mean = grouped(jnp.sum(sums, axis=0, keepdims=True)) / all_count
    gap0 = stat[:, 0, :] / counts - mean
    gap1 = stat[:, 2, :] / counts - mean
    spread = stat[:, 1, :] + stat[:, 3, :] + (gap0 * gap0 + gap1 * gap1) * counts
    var = grouped(jnp.sum(spread, axis=0, keepdims=True)) / all_count
    scale = gain_ref[...] * lax.rsqrt(var + 1e-5)
    mul = 0.5 * scale
    add = 0.5 * (bias_ref[...] - mean * scale)
    stores = []
    for step in range(valid_ref.shape[0] // frames):
        live = valid_rows(step * frames, valid_ref[me], frames, rows)
        here = pl.ds(step * m, m)
        cut = far0_ref.shape[1]
        there = pl.ds(step * m % cut, m)
        late_ref = far1_ref if step * m >= cut else far0_ref
        for y in range(2):
            line = 1 - odd if y == 0 else odd
            for b in range(2):
                if y == 0:
                    half = near_ref[b, here] * mul + add
                else:
                    half = late_ref[b, there] * mul + add
                z = jnp.where(live, half + half * jnp.tanh(half), 0.0)
                for c in range(channels // 128):
                    mix_ref[y, c, pl.ds(b, m, 2), :] = z[:, 128 * c : 128 * (c + 1)]
            for f in range(frames):
                for c in range(channels // 128):
                    out_ref[step * frames + f, line, :, 128 * c : 128 * (c + 1)] = mix_ref[
                        y, c, 2 * rows * f : 2 * rows * (f + 1), :
                    ].astype(BF)
        now = pl.ds(step * frames, frames)
        stores.append(pltpu.make_async_copy(out_ref.at[now], out_hbm.at[now], sems.at[step]))
        stores[-1].start()
    for copy in stores:
        copy.wait()


def norm(rows, me, valid, stat, gain, bias, near_plane, *far_planes):
    count, channels = near_plane.shape[1:]
    n = valid.shape[0]
    frames = n // 4
    m = frames * rows
    smem = pl.BlockSpec(memory_space=pltpu.SMEM)
    return pl.pallas_call(
        functools.partial(norm_kernel, rows, channels // NORM_GROUPS, frames),
        in_specs=[smem, smem] + [INSIDE] * 6,
        out_specs=HBM,
        scratch_shapes=[
            pltpu.VMEM((2, channels // 128, 2 * m, 128), F32),
            pltpu.VMEM((n, 2, 2 * rows, channels), BF),
            pltpu.SemaphoreType.DMA((n // frames,)),
        ],
        out_shape=pltpu.HBM((n, 2, 2 * rows, channels), BF),
        compiler_params=pltpu.CompilerParams(vmem_limit_bytes=24 * MIB),
        cost_estimate=cost(32 * count * channels, 24 * count * channels, 4 * count * channels),
    )(
        me, valid, stat, gain.reshape(1, channels), bias.reshape(1, channels), near_plane, *far_planes
    )


def local(
    tokens,
    qkv_weight,
    out_weight,
    conv_weight,
    norm_gain,
    norm_bias,
    group_map,
    token_order,
    valid_frames,
):
    tiles = lax.axis_size("tm")
    rank = lax.axis_index("tm")
    count, width = tokens.shape
    rows = count // tiles
    channels = conv_weight.shape[3]
    head = width // HEADS
    me = rank.reshape(1).astype(jnp.int32)

    def swap(x, pairs):
        return lax.ppermute(x, "tm", pairs)

    qkv_weight, out_weight, taps = (
        pltpu.with_memory_space_constraint(w, pltpu.HBM)
        for w in (qkv_weight, out_weight, conv_weight.reshape(-1, channels))
    )
    raster = permute(token_order, tokens)
    tile = lax.all_to_all(
        raster.reshape(tiles, rows, width), "tm", split_axis=0, concat_axis=0, tiled=True
    ).reshape(count, width)
    buf, wq, wo, w2, wx = run_state(me, tokens, qkv_weight, out_weight, taps, head)

    def swap_by(x, k):
        return swap(x, [(i, i ^ k) for i in range(tiles)])

    k, gate = 2, None
    while k < tiles:
        ks = [k] if k == 2 or 2 * k >= tiles else [k, 2 * k, 3 * k]
        got = [swap_by(buf, ks[0])]
        late, _ = lax.optimization_barrier((buf, got[0]))
        got += [swap_by(late, j) for j in ks[1:]]
        gate = got[0]
        buf = jnp.concatenate([buf] + got, axis=0)
        k *= 2 if len(ks) == 1 else 4
    pieces = [buf, swap_by(buf, 1)]
    tile, _ = lax.optimization_barrier((tile, gate))
    inner = swap_by(tile, 1)
    ends = [(i, i + 1) for i in range(1, tiles - 1, 2)]
    ends = ends + [(j, i) for i, j in ends]
    cut = count // 2
    outer = [swap(tile[:cut], ends), swap(tile[cut:], ends)]
    near_plane, part, state, total, near_stat = near(
        rows, me, group_map, valid_frames, pieces, tile, inner, (wq, wo, w2, taps),
        channels, head,
    )
    stat, planes = jnp.zeros((8, channels), F32), []
    for i, piece in enumerate(outer):
        plane, stat = far(
            rows, i * tiles // 2, me, valid_frames, piece, state, total, part, stat, near_stat,
            (wq, wo, wx),
        )
        planes.append(plane)
    stat = lax.all_to_all(stat, "tm", split_axis=0, concat_axis=0, tiled=True)
    return norm(rows, me, valid_frames, stat, norm_gain, norm_bias, near_plane, *planes)


def solution(mesh):
    in_specs = (P(("clip", "tm"), None), P(), P(), P(), P(), P(), P("clip"), P("clip"), P("clip"))
    out_specs = P("clip", "tm", None, None)
    return jax.shard_map(local, mesh=mesh, in_specs=in_specs, out_specs=out_specs, check_vma=False)
```

```python
import functools

import jax
import jax.numpy as jnp
from jax import lax
from jax.experimental import pallas as pl
from jax.experimental.pallas import tpu as pltpu
from jax.sharding import PartitionSpec as P

HEADS = 16
NORM_GROUPS = 32
BF = jnp.bfloat16
F32 = jnp.float32
MIB = 1024 * 1024
VMEM = 60
HBM = pl.BlockSpec(memory_space=pltpu.HBM)
ANY = pl.BlockSpec(memory_space=pl.ANY)
INSIDE = pl.BlockSpec(memory_space=pltpu.VMEM)


def dot(a, b, **kw):
    return jnp.dot(a, b, preferred_element_type=F32, **kw)


def params(mib, dims=1):
    return pltpu.CompilerParams(
        vmem_limit_bytes=mib * MIB, dimension_semantics=("arbitrary",) * dims
    )


def cost(flops, nbytes, trans=0):
    return pl.CostEstimate(flops=int(flops), bytes_accessed=int(nbytes), transcendentals=int(trans))


def same_block(shape, size):
    rows = lax.broadcasted_iota(jnp.int32, shape, 0) // size
    cols = lax.broadcasted_iota(jnp.int32, shape, 1) // size
    return rows == cols


def permute_kernel(order_any, tok_any, out_any, order_ref, tok_ref, pick_ref, out_ref, sems):
    count, width = tok_ref.shape
    parts = sems.shape[0] - 2
    rows = count // parts
    loads = [
        pltpu.make_async_copy(order_any, order_ref, sems.at[0]),
        pltpu.make_async_copy(tok_any, tok_ref, sems.at[1]),
    ]
    for copy in loads:
        copy.start()
    loads[0].wait()
    place = lax.broadcasted_iota(jnp.int32, (count, count), 0)
    pick_ref[...] = jnp.where(place == order_ref[...], 1.0, 0.0).astype(BF)
    loads[1].wait()
    stores = []
    for i in range(parts):
        cut = pl.ds(i * rows, rows)
        out_ref[cut] = dot(pick_ref[cut], tok_ref[...]).astype(BF)
        stores.append(pltpu.make_async_copy(out_ref.at[cut], out_any.at[cut], sems.at[2 + i]))
        stores[-1].start()
    for copy in stores:
        copy.wait()


def permute(order, tokens):
    count, width = tokens.shape
    parts = 4
    return pl.pallas_call(
        permute_kernel,
        in_specs=[HBM, HBM],
        out_specs=HBM,
        out_shape=pltpu.HBM((count, width), BF),
        scratch_shapes=[
            pltpu.VMEM((1, count), jnp.int32),
            pltpu.VMEM((count, width), BF),
            pltpu.VMEM((count, count), BF),
            pltpu.VMEM((count, width), BF),
            pltpu.SemaphoreType.DMA((2 + parts,)),
        ],
        compiler_params=pltpu.CompilerParams(vmem_limit_bytes=60 * MIB),
        cost_estimate=cost(2 * count * count * width, 4 * count * width),
    )(order.reshape(1, count), tokens)


def chunk(src, dst, step, m, sem):
    at = pl.ds(pl.multiple_of(step * m, m), m)
    return pltpu.make_async_copy(src.at[at], dst.at[at], sem.at[step])


def spread_row(src, row, dst, sems):
    deep, channels = dst.shape[0] * 3 // 4, dst.shape[1] // 2
    part = src.at[pl.ds(pl.multiple_of(row * deep, deep), deep), :]
    return [
        pltpu.make_async_copy(part, dst.at[:deep, :channels], sems.at[0]),
        pltpu.make_async_copy(part, dst.at[channels:, channels:], sems.at[1]),
    ]


def clear_spread(dst):
    channels = dst.shape[1] // 2
    gap = jnp.zeros((channels, channels), BF)
    dst[3 * channels :, :channels] = gap
    dst[:channels, channels:] = gap


def state_kernel(
    head, pos_ref, tok_ref, wk_ref, wv_ref, qkv_hbm, wo_hbm, taps_hbm,
    out_ref, wq_ref, wo_ref, w2_ref, wx_ref,
    acc_ref, sum_ref, sems,
):
    step = pl.program_id(0)
    odd = jnp.bitwise_and(pos_ref[0], 1)
    channels = taps_hbm.shape[1]
    row = 3 * channels
    first_half = taps_hbm.at[pl.ds(pl.multiple_of(odd * row, row), 2 * row), :]
    second_half = taps_hbm.at[pl.ds(pl.multiple_of((1 - odd) * row, row), 2 * row), :]
    staged = [
        pltpu.make_async_copy(qkv_hbm.at[:, pl.ds(0, wq_ref.shape[1])], wq_ref, sems.at[0]),
        pltpu.make_async_copy(wo_hbm, wo_ref, sems.at[1]),
        pltpu.make_async_copy(first_half, w2_ref.at[:, :channels], sems.at[2]),
        pltpu.make_async_copy(second_half, w2_ref.at[:, channels:], sems.at[3]),
    ]
    staged += spread_row(taps_hbm, 2 * odd, wx_ref, sems.at[pl.ds(4, 2)])
    width = tok_ref.shape[1]
    block = acc_ref.shape[1]

    @pl.when(step == 0)
    def _():
        acc_ref[...] = jnp.zeros_like(acc_ref)
        sum_ref[...] = jnp.zeros_like(sum_ref)
        for copy in staged:
            copy.start()
        clear_spread(wx_ref)

    tok = tok_ref[...]
    keys = jnp.maximum(dot(tok, wk_ref[...]), 0.0)
    keys_b = keys.astype(BF)
    vals_b = dot(tok, wv_ref[...]).astype(BF)
    sum_ref[0:1, :] += jnp.sum(keys_b.astype(F32), axis=0, keepdims=True)
    for i in range(width // block):
        cut = slice(i * block, (i + 1) * block)
        acc_ref[i] += lax.dot_general(
            keys_b[:, cut], vals_b[:, cut], (((0,), (0,)), ((), ())), preferred_element_type=F32
        )

    @pl.when(step == pl.num_programs(0) - 1)
    def _():
        own = same_block((block, block), head)
        parts = []
        for i in range(width // block):
            full = jnp.where(own, acc_ref[i], 0.0)
            small = full[:head]
            for h in range(1, block // head):
                small = small + full[h * head : (h + 1) * head]
            parts.append(small)
        state = jnp.concatenate(parts, axis=1)
        total = sum_ref[0:1, :]
        high = total.astype(BF).astype(F32)
        low = total - high
        lines = [row[:, 128 * i : 128 * (i + 1)] for row in (high, low) for i in range(width // 128)]
        rows = out_ref.shape[1]
        lines.append(jnp.zeros((rows - len(lines), 128), F32))
        cuts = [state[i : i + rows] for i in range(0, head, rows)]
        for copy in staged:
            copy.wait()
        out_ref[0] = jnp.concatenate(cuts + [jnp.concatenate(lines, axis=0)], axis=1).astype(BF)


def unpack(packed, head, width):
    rows = packed.shape[0]
    cuts = head // rows
    state = jnp.concatenate([packed[:, i * width : (i + 1) * width] for i in range(cuts)], axis=0)
    tail = packed[:, cuts * width :]
    lines = width // 128
    both = tail[:lines] + tail[lines : 2 * lines]
    return state, jnp.concatenate([both[i : i + 1] for i in range(lines)], axis=1)


def run_state(me, tokens, qkv_weight, out_weight, taps, head):
    count, width = tokens.shape
    steps, block = 4, 256
    rows = 16
    packed = head // rows * width + 128
    channels = taps.shape[1]
    return pl.pallas_call(
        functools.partial(state_kernel, head),
        grid=(steps,),
        in_specs=[
            pl.BlockSpec(memory_space=pltpu.SMEM),
            pl.BlockSpec((count // steps, width), lambda i: (i, 0)),
            pl.BlockSpec((width, width), lambda i: (0, 1)),
            pl.BlockSpec((width, width), lambda i: (0, 2)),
            HBM,
            HBM,
            HBM,
        ],
        out_specs=[pl.BlockSpec((1, rows, packed), lambda i: (0, 0, 0))] + [INSIDE] * 4,
        out_shape=[
            jax.ShapeDtypeStruct((1, rows, packed), BF),
            pltpu.VMEM((width, width), BF),
            pltpu.VMEM(out_weight.shape, BF),
            pltpu.VMEM((6 * channels, 2 * channels), BF),
            pltpu.VMEM((4 * channels, 2 * channels), BF),
        ],
        scratch_shapes=[
            pltpu.VMEM((width // block, block, block), F32),
            pltpu.VMEM((8, width), F32),
            pltpu.SemaphoreType.DMA((6,)),
        ],
        compiler_params=params(16),
        cost_estimate=cost(4 * count * width * width, 8 * count * width),
    )(me, tokens, qkv_weight, qkv_weight, qkv_weight, out_weight, taps)


def queries(tok, wq):
    return jnp.maximum(dot(tok, wq).astype(BF).astype(F32), 0.0)


def attend(qf, state, total, own, ones):
    block = own.shape[0]
    head, width = state.shape
    qb = qf.astype(BF)
    den_in = (qf * total).astype(BF)
    outs = []
    for i in range(width // block):
        cut = slice(i * block, (i + 1) * block)
        wide = jnp.concatenate([state[:, cut]] * (block // head), axis=0)
        wide = jnp.where(own, wide, jnp.zeros_like(wide))
        numer = dot(qb[:, cut], wide)
        denom = dot(den_in[:, cut], ones) + 1.0
        outs.append(numer / denom)
    return jnp.concatenate(outs, axis=1)


def valid_rows(first, limit, frames, rows):
    frame = lax.broadcasted_iota(jnp.int32, (frames * rows, 1), 0) // rows + first
    return frame < limit


def store_taps(x_ref, at, line, rows):
    m, channels = line.shape[0], line.shape[1] // 2
    column = lax.broadcasted_iota(jnp.int32, (m, 1), 0) % rows
    even_px, odd_px = line[:, :channels], line[:, channels:]
    left = jnp.where(column == 0, 0.0, pltpu.roll(odd_px, 1, 0))
    right = jnp.where(column == rows - 1, 0.0, pltpu.roll(even_px, m - 1, 0))
    for b, taps in enumerate(((left, even_px, odd_px), (even_px, odd_px, right))):
        for d, tap in enumerate(taps):
            cut = slice(at + d * channels, at + (d + 1) * channels)
            x_ref[b * m : (b + 1) * m, cut] = tap.astype(BF)


def line_taps(line, rows):
    m, channels = line.shape[0], line.shape[1] // 2
    column = lax.broadcasted_iota(jnp.int32, (m, 1), 0) % rows
    even_px, odd_px = line[:, :channels], line[:, channels:]
    left = jnp.where(column == 0, 0.0, pltpu.roll(odd_px, 1, 0))
    right = jnp.where(column == rows - 1, 0.0, pltpu.roll(even_px, m - 1, 0))
    return jnp.concatenate([left.astype(BF), line.astype(BF), right.astype(BF)], axis=1)


def gather_stats(run_ref, res, live, limit, first, frames, rows):
    part = jnp.sum(res, axis=0, keepdims=True)
    count = (jnp.clip(limit - first, 0, frames) * (2 * rows)).astype(F32)
    mean = part / jnp.maximum(count, 1.0)
    dev = jnp.where(live, res - mean, 0.0)
    spread = jnp.sum(dev * dev, axis=0, keepdims=True)
    had = (jnp.clip(limit, 0, first) * (2 * rows)).astype(F32)
    run_sum = run_ref[0:1, :]
    gap = mean - run_sum / jnp.maximum(had, 1.0)
    weight = had * count / jnp.maximum(had + count, 1.0)
    run_ref[1:2, :] += spread + gap * gap * weight
    run_ref[0:1, :] = run_sum + part


def near_kernel(
    rows, parts, frames, pos_ref, group_ref, valid_ref, *refs
):
    pieces, refs = refs[: 2 * parts], refs[2 * parts :]
    own_any, inner_any, wq_ref, wo_ref, w2_ref, taps_hbm, *refs = refs
    near_ref, part_ref, state_ref, total_ref, stat_ref, *refs = refs
    acc_ref, pend_ref, att_ref, x_ref, w1_ref, own_ref, inner_ref, buf_ref, *refs = refs
    own_sem, inner_sem, piece_sem, sems = refs
    late = spread_row(taps_hbm, 2 - 2 * jnp.bitwise_and(pos_ref[0], 1), w1_ref, sems)
    step = pl.program_id(0)
    count, width = own_ref.shape
    m = frames * rows
    steps = count // m
    me = pos_ref[0]
    odd = jnp.bitwise_and(me, 1)
    head = state_ref.shape[1]
    channels = near_ref.shape[2]
    size = pieces[0].shape[0]
    fetch = [
        pltpu.make_async_copy(
            pieces[i], buf_ref.at[i // parts, pl.ds(i % parts * size, size)], piece_sem.at[i]
        )
        for i in range(2 * parts)
    ]

    @pl.when(step == 0)
    def _():
        for copy in fetch:
            copy.start()
        for i in range(steps):
            chunk(own_any, own_ref, i, m, own_sem).start()
            chunk(inner_any, inner_ref, i, m, inner_sem).start()
        for copy in late:
            copy.start()
        clear_spread(w1_ref)
        acc_ref[...] = jnp.zeros_like(acc_ref)
        pend_ref[...] = jnp.zeros_like(pend_ref)
        stat_ref[...] = jnp.zeros_like(stat_ref)
        for copy in fetch:
            copy.wait()

    chunk(own_any, own_ref, step, m, own_sem).wait()
    chunk(inner_any, inner_ref, step, m, inner_sem).wait()
    here = pl.ds(pl.multiple_of(step * m, m), m)
    block = 256
    own = same_block((block, block), head)
    ones = jnp.where(own, 1.0, 0.0).astype(BF)
    wq = wq_ref[...]
    q_own = queries(own_ref[here, :], wq)
    q_inner = queries(inner_ref[here, :], wq)
    for i in range(frames):
        frame = step * frames + i
        rel = jnp.bitwise_xor(frame, me)
        piece = buf_ref[jnp.bitwise_and(rel, 1), rel // 2].astype(F32)
        before = group_ref[jnp.maximum(frame - 1, 0)]
        fresh = jnp.where(group_ref[frame] != before, 1.0, 0.0)
        pend = pend_ref[...]
        acc = acc_ref[...] + fresh * pend
        acc_ref[...] = acc
        pend_ref[...] = (1.0 - fresh) * pend + piece
        summed = acc + piece
        state, total = unpack(summed, head, width)
        state = state.astype(BF)
        state_ref[frame] = state
        total_ref[frame] = jnp.broadcast_to(total, (8, width))
        cut = slice(i * rows, (i + 1) * rows)
        both = jnp.concatenate([q_own[cut], q_inner[cut]], axis=0)
        res = attend(both, state, total, own, ones)
        att_ref[0, cut] = res[:rows]
        att_ref[1, cut] = res[rows:]
    first = step * frames
    limit = valid_ref[me]
    keep_own = valid_rows(first, limit, frames, rows)
    keep_inner = valid_rows(first, valid_ref[jnp.bitwise_xor(me, 1)], frames, rows)

    @pl.when(step == 0)
    def _():
        for copy in late:
            copy.wait()

    half, row = 2 * channels, 3 * channels
    mine = jnp.where(keep_own, dot(att_ref[0].astype(BF), wo_ref[...]), 0.0)
    w_close = wo_ref[:, pl.ds(pl.multiple_of(odd * half, half), half)]
    close = jnp.where(keep_inner, dot(att_ref[1].astype(BF), w_close), 0.0)
    store_taps(x_ref, 0, mine[:, : 2 * channels], rows)
    store_taps(x_ref, row, mine[:, 2 * channels :], rows)
    live = jnp.concatenate([keep_own, keep_own], axis=0)
    pair = dot(x_ref[...], w2_ref[...])
    more = dot(line_taps(close, rows), w1_ref[...])
    more = jnp.concatenate([more[:, :channels], more[:, channels:]], axis=0)
    res = jnp.where(live, pair[:, :channels] + more, 0.0)
    near_ref[0, here] = res[:m]
    near_ref[1, here] = res[m:]
    gather_stats(stat_ref, res, live, limit, first, frames, rows)
    part_ref[0, here] = pair[:m, channels:]
    part_ref[1, here] = pair[m:, channels:]


def near(rows, me, group_map, valid, pieces, own, inner, weights, channels, head):
    count, width = own.shape
    frames = 16
    n = count // rows
    m = frames * rows
    deep, packed = pieces[0].shape[1:]
    parts = len(pieces) // 2
    return pl.pallas_call(
        functools.partial(near_kernel, rows, parts, frames),
        grid_spec=pltpu.PrefetchScalarGridSpec(
            num_scalar_prefetch=3,
            grid=(n // frames,),
            in_specs=[ANY] * (2 * parts + 2) + [INSIDE] * 3 + [HBM],
            out_specs=[INSIDE] * 5,
            scratch_shapes=[
                pltpu.VMEM((deep, packed), F32),
                pltpu.VMEM((deep, packed), F32),
                pltpu.VMEM((2, m, width), F32),
                pltpu.VMEM((2 * m, 6 * channels), BF),
                pltpu.VMEM((4 * channels, 2 * channels), BF),
                pltpu.VMEM((count, width), BF),
                pltpu.VMEM((count, width), BF),
                pltpu.VMEM((2, n // 2, deep, packed), BF),
                pltpu.SemaphoreType.DMA((n // frames,)),
                pltpu.SemaphoreType.DMA((n // frames,)),
                pltpu.SemaphoreType.DMA((2 * parts,)),
                pltpu.SemaphoreType.DMA((2,)),
            ],
        ),
        out_shape=[
            pltpu.VMEM((2, count, channels), F32),
            pltpu.VMEM((2, count, channels), F32),
            pltpu.VMEM((n, head, width), BF),
            pltpu.VMEM((n, 8, width), F32),
            pltpu.VMEM((8, channels), F32),
        ],
        compiler_params=params(32),
        cost_estimate=cost(1, 1),
    )(me, group_map, valid, *pieces, own, inner, *weights)


def far_kernel(
    rows, first, last, pos_ref, valid_ref,
    outer_any, state_ref, total_ref, part_ref, before_ref, near_stat_ref, wq_ref, wo_ref, wx_ref,
    far_ref, stat_ref,
    att_ref, run_ref, outer_ref, sem,
):
    m, width = outer_ref.shape
    channels = far_ref.shape[2]
    frames = m // rows
    me = pos_ref[0]
    odd = jnp.bitwise_and(me, 1)
    head = state_ref.shape[1]
    half = 2 * channels
    half_at = pl.ds(pl.multiple_of((1 - odd) * half, half), half)
    copy = pltpu.make_async_copy(outer_any, outer_ref, sem)
    copy.start()
    run_ref[...] = before_ref[...]
    block = 256
    own = same_block((block, block), head)
    ones = jnp.where(own, 1.0, 0.0).astype(BF)
    copy.wait()
    qf = queries(outer_ref[...], wq_ref[...])
    for i in range(frames):
        cut = slice(i * rows, (i + 1) * rows)
        frame = first + i
        att_ref[cut] = attend(qf[cut], state_ref[frame], total_ref[frame][0:1], own, ones)
    outer_at = jnp.clip(me + 2 * odd - 1, 0, valid_ref.shape[0] - 1)
    keep = valid_rows(first, valid_ref[outer_at], frames, rows)
    line = jnp.where(keep, dot(att_ref[...].astype(BF), wo_ref[:, half_at]), 0.0)
    more = dot(line_taps(line, rows), wx_ref[...])
    more = jnp.concatenate([more[:, :channels], more[:, channels:]], axis=0)
    limit = valid_ref[me]
    live = valid_rows(first, limit, frames, rows)
    live = jnp.concatenate([live, live], axis=0)
    here = pl.ds(first * rows, m)
    part = jnp.concatenate([part_ref[0, here], part_ref[1, here]], axis=0)
    res = jnp.where(live, part + more, 0.0)
    far_ref[0] = res[:m]
    far_ref[1] = res[m:]
    gather_stats(run_ref, res, live, limit, first, frames, rows)
    if last:
        both = jnp.concatenate([near_stat_ref[0:2], run_ref[0:2], run_ref[4:8]], axis=0)
        stat_ref[...] = jnp.broadcast_to(both[None], stat_ref.shape)
    else:
        stat_ref[...] = run_ref[...]


def far(rows, first, me, valid, outer, state, total, part, before, near_stat, weights):
    m, width = outer.shape
    channels = part.shape[2]
    n = state.shape[0]
    last = first + m // rows == n
    smem = pl.BlockSpec(memory_space=pltpu.SMEM)
    stat = jax.ShapeDtypeStruct((n, 8, channels), F32) if last else pltpu.VMEM((8, channels), F32)
    return pl.pallas_call(
        functools.partial(far_kernel, rows, first, last),
        in_specs=[smem, smem, ANY] + [INSIDE] * 8,
        out_specs=[INSIDE, INSIDE],
        scratch_shapes=[
            pltpu.VMEM((m, width), F32),
            pltpu.VMEM((8, channels), F32),
            pltpu.VMEM((m, width), BF),
            pltpu.SemaphoreType.DMA,
        ],
        out_shape=[pltpu.VMEM((2, m, channels), F32), stat],
        compiler_params=pltpu.CompilerParams(vmem_limit_bytes=16 * MIB),
        cost_estimate=cost(1, 1),
    )(me, valid, outer, state, total, part, before, near_stat, *weights)


def norm_kernel(
    rows, size, frames, pos_ref, valid_ref, stat_ref, gain_ref, bias_ref, near_ref, far0_ref, far1_ref,
    out_hbm, mix_ref, out_ref, sems,
):
    m = frames * rows
    channels = out_ref.shape[3]
    me = pos_ref[0]
    odd = jnp.bitwise_and(me, 1)

    stat = stat_ref[...]
    tile = lax.broadcasted_iota(jnp.int32, (stat.shape[0], channels), 0)
    counts = jnp.zeros(tile.shape, F32)
    for i in range(stat.shape[0]):
        counts = jnp.where(tile == i, (valid_ref[i] * (2 * rows)).astype(F32), counts)
    mix = jnp.where(same_block((channels, channels), size), 1.0, 0.0)
    all_count = jnp.sum(counts, axis=0, keepdims=True) * (2 * size)

    def grouped(row):
        wide = jnp.broadcast_to(row, (8, channels))
        return dot(wide, mix, precision=lax.Precision.HIGHEST)[0:1]

    sums = stat[:, 0, :] + stat[:, 2, :]
    mean = grouped(jnp.sum(sums, axis=0, keepdims=True)) / all_count
    gap0 = stat[:, 0, :] / counts - mean
    gap1 = stat[:, 2, :] / counts - mean
    spread = stat[:, 1, :] + stat[:, 3, :] + (gap0 * gap0 + gap1 * gap1) * counts
    var = grouped(jnp.sum(spread, axis=0, keepdims=True)) / all_count
    scale = gain_ref[...] * lax.rsqrt(var + 1e-5)
    mul = 0.5 * scale
    add = 0.5 * (bias_ref[...] - mean * scale)
    stores = []
    for step in range(valid_ref.shape[0] // frames):
        live = valid_rows(step * frames, valid_ref[me], frames, rows)
        here = pl.ds(step * m, m)
        cut = far0_ref.shape[1]
        there = pl.ds(step * m % cut, m)
        late_ref = far1_ref if step * m >= cut else far0_ref
        for y in range(2):
            line = 1 - odd if y == 0 else odd
            for b in range(2):
                if y == 0:
                    half = near_ref[b, here] * mul + add
                else:
                    half = late_ref[b, there] * mul + add
                z = jnp.where(live, half + half * jnp.tanh(half), 0.0)
                for c in range(channels // 128):
                    mix_ref[y, c, pl.ds(b, m, 2), :] = z[:, 128 * c : 128 * (c + 1)]
            for f in range(frames):
                for c in range(channels // 128):
                    out_ref[step * frames + f, line, :, 128 * c : 128 * (c + 1)] = mix_ref[
                        y, c, 2 * rows * f : 2 * rows * (f + 1), :
                    ].astype(BF)
        now = pl.ds(step * frames, frames)
        stores.append(pltpu.make_async_copy(out_ref.at[now], out_hbm.at[now], sems.at[step]))
        stores[-1].start()
    for copy in stores:
        copy.wait()


def norm(rows, me, valid, stat, gain, bias, near_plane, *far_planes):
    count, channels = near_plane.shape[1:]
    n = valid.shape[0]
    frames = n // 4
    m = frames * rows
    smem = pl.BlockSpec(memory_space=pltpu.SMEM)
    return pl.pallas_call(
        functools.partial(norm_kernel, rows, channels // NORM_GROUPS, frames),
        in_specs=[smem, smem] + [INSIDE] * 6,
        out_specs=HBM,
        scratch_shapes=[
            pltpu.VMEM((2, channels // 128, 2 * m + 8, 128), F32),
            pltpu.VMEM((n, 2, 2 * rows, channels), BF),
            pltpu.SemaphoreType.DMA((n // frames,)),
        ],
        out_shape=pltpu.HBM((n, 2, 2 * rows, channels), BF),
        compiler_params=pltpu.CompilerParams(vmem_limit_bytes=24 * MIB),
        cost_estimate=cost(32 * count * channels, 24 * count * channels, 4 * count * channels),
    )(
        me, valid, stat, gain.reshape(1, channels), bias.reshape(1, channels), near_plane, *far_planes
    )


def local(
    tokens,
    qkv_weight,
    out_weight,
    conv_weight,
    norm_gain,
    norm_bias,
    group_map,
    token_order,
    valid_frames,
):
    tiles = lax.axis_size("tm")
    rank = lax.axis_index("tm")
    count, width = tokens.shape
    rows = count // tiles
    channels = conv_weight.shape[3]
    head = width // HEADS
    me = rank.reshape(1).astype(jnp.int32)

    def swap(x, pairs):
        return lax.ppermute(x, "tm", pairs)

    qkv_weight, out_weight, taps = (
        pltpu.with_memory_space_constraint(w, pltpu.HBM)
        for w in (qkv_weight, out_weight, conv_weight.reshape(-1, channels))
    )
    raster = permute(token_order, tokens)
    tile = lax.all_to_all(
        raster.reshape(tiles, rows, width), "tm", split_axis=0, concat_axis=0, tiled=True
    ).reshape(count, width)
    buf, wq, wo, w2, wx = run_state(me, tokens, qkv_weight, out_weight, taps, head)

    def swap_by(x, k):
        return swap(x, [(i, i ^ k) for i in range(tiles)])

    k, gate = 2, None
    while k < tiles:
        ks = [k] if k == 2 or 2 * k >= tiles else [k, 2 * k, 3 * k]
        got = [swap_by(buf, ks[0])]
        late, _ = lax.optimization_barrier((buf, got[0]))
        got += [swap_by(late, j) for j in ks[1:]]
        gate = got[0]
        buf = jnp.concatenate([buf] + got, axis=0)
        k *= 2 if len(ks) == 1 else 4
    pieces = [buf, swap_by(buf, 1)]
    tile, _ = lax.optimization_barrier((tile, gate))
    inner = swap_by(tile, 1)
    ends = [(i, i + 1) for i in range(1, tiles - 1, 2)]
    ends = ends + [(j, i) for i, j in ends]
    cut = count // 4 * 3
    outer = [swap(tile[:cut], ends), swap(tile[cut:], ends)]
    near_plane, part, state, total, near_stat = near(
        rows, me, group_map, valid_frames, pieces, tile, inner, (wq, wo, w2, taps),
        channels, head,
    )
    stat, planes = jnp.zeros((8, channels), F32), []
    for i, piece in enumerate(outer):
        plane, stat = far(
            rows, i * cut // rows, me, valid_frames, piece, state, total, part, stat, near_stat,
            (wq, wo, wx),
        )
        planes.append(plane)
    stat = lax.all_to_all(stat, "tm", split_axis=0, concat_axis=0, tiled=True)
    return norm(rows, me, valid_frames, stat, norm_gain, norm_bias, near_plane, *planes)


def solution(mesh):
    in_specs = (P(("clip", "tm"), None), P(), P(), P(), P(), P(), P("clip"), P("clip"), P("clip"))
    out_specs = P("clip", "tm", None, None)
    return jax.shard_map(local, mesh=mesh, in_specs=in_specs, out_specs=out_specs, check_vma=False)
```

```python
import functools

import jax
import jax.numpy as jnp
from jax import lax
from jax.experimental import pallas as pl
from jax.experimental.pallas import tpu as pltpu
from jax.sharding import PartitionSpec as P

HEADS = 16
NORM_GROUPS = 32
BF = jnp.bfloat16
F32 = jnp.float32
MIB = 1024 * 1024
VMEM = 60
HBM = pl.BlockSpec(memory_space=pltpu.HBM)
ANY = pl.BlockSpec(memory_space=pl.ANY)
INSIDE = pl.BlockSpec(memory_space=pltpu.VMEM)


def dot(a, b, **kw):
    return jnp.dot(a, b, preferred_element_type=F32, **kw)


def params(mib, dims=1):
    return pltpu.CompilerParams(
        vmem_limit_bytes=mib * MIB, dimension_semantics=("arbitrary",) * dims
    )


def cost(flops, nbytes, trans=0):
    return pl.CostEstimate(flops=int(flops), bytes_accessed=int(nbytes), transcendentals=int(trans))


def same_block(shape, size):
    rows = lax.broadcasted_iota(jnp.int32, shape, 0) // size
    cols = lax.broadcasted_iota(jnp.int32, shape, 1) // size
    return rows == cols


def permute_kernel(order_any, tok_any, out_any, order_ref, tok_ref, pick_ref, out_ref, sems):
    count, width = tok_ref.shape
    parts = sems.shape[0] - 2
    rows = count // parts
    loads = [
        pltpu.make_async_copy(order_any, order_ref, sems.at[0]),
        pltpu.make_async_copy(tok_any, tok_ref, sems.at[1]),
    ]
    for copy in loads:
        copy.start()
    loads[0].wait()
    place = lax.broadcasted_iota(jnp.int32, (count, count), 0)
    pick_ref[...] = jnp.where(place == order_ref[...], 1.0, 0.0).astype(BF)
    loads[1].wait()
    stores = []
    for i in range(parts):
        cut = pl.ds(i * rows, rows)
        out_ref[cut] = dot(pick_ref[cut], tok_ref[...]).astype(BF)
        stores.append(pltpu.make_async_copy(out_ref.at[cut], out_any.at[cut], sems.at[2 + i]))
        stores[-1].start()
    for copy in stores:
        copy.wait()


def permute(order, tokens):
    count, width = tokens.shape
    parts = 4
    return pl.pallas_call(
        permute_kernel,
        in_specs=[HBM, HBM],
        out_specs=HBM,
        out_shape=pltpu.HBM((count, width), BF),
        scratch_shapes=[
            pltpu.VMEM((1, count), jnp.int32),
            pltpu.VMEM((count, width), BF),
            pltpu.VMEM((count, count), BF),
            pltpu.VMEM((count, width), BF),
            pltpu.SemaphoreType.DMA((2 + parts,)),
        ],
        compiler_params=pltpu.CompilerParams(vmem_limit_bytes=60 * MIB),
        cost_estimate=cost(2 * count * count * width, 4 * count * width),
    )(order.reshape(1, count), tokens)


def chunk(src, dst, step, m, sem):
    at = pl.ds(pl.multiple_of(step * m, m), m)
    return pltpu.make_async_copy(src.at[at], dst.at[at], sem.at[step])


def spread_row(src, row, dst, sems):
    deep, channels = dst.shape[0] * 3 // 4, dst.shape[1] // 2
    part = src.at[pl.ds(pl.multiple_of(row * deep, deep), deep), :]
    return [
        pltpu.make_async_copy(part, dst.at[:deep, :channels], sems.at[0]),
        pltpu.make_async_copy(part, dst.at[channels:, channels:], sems.at[1]),
    ]


def clear_spread(dst):
    channels = dst.shape[1] // 2
    gap = jnp.zeros((channels, channels), BF)
    dst[3 * channels :, :channels] = gap
    dst[:channels, channels:] = gap


def state_kernel(
    head, pos_ref, tok_ref, wk_ref, wv_ref, qkv_hbm, wo_hbm, taps_hbm,
    out_ref, wq_ref, wo_ref, w2_ref, wx_ref,
    acc_ref, sum_ref, sems,
):
    step = pl.program_id(0)
    odd = jnp.bitwise_and(pos_ref[0], 1)
    channels = taps_hbm.shape[1]
    row = 3 * channels
    first_half = taps_hbm.at[pl.ds(pl.multiple_of(odd * row, row), 2 * row), :]
    second_half = taps_hbm.at[pl.ds(pl.multiple_of((1 - odd) * row, row), 2 * row), :]
    staged = [
        pltpu.make_async_copy(qkv_hbm.at[:, pl.ds(0, wq_ref.shape[1])], wq_ref, sems.at[0]),
        pltpu.make_async_copy(wo_hbm, wo_ref, sems.at[1]),
        pltpu.make_async_copy(first_half, w2_ref.at[:, :channels], sems.at[2]),
        pltpu.make_async_copy(second_half, w2_ref.at[:, channels:], sems.at[3]),
    ]
    staged += spread_row(taps_hbm, 2 * odd, wx_ref, sems.at[pl.ds(4, 2)])
    width = tok_ref.shape[1]
    block = acc_ref.shape[1]

    @pl.when(step == 0)
    def _():
        acc_ref[...] = jnp.zeros_like(acc_ref)
        sum_ref[...] = jnp.zeros_like(sum_ref)
        for copy in staged:
            copy.start()
        clear_spread(wx_ref)

    tok = tok_ref[...]
    keys = jnp.maximum(dot(tok, wk_ref[...]), 0.0)
    keys_b = keys.astype(BF)
    vals_b = dot(tok, wv_ref[...]).astype(BF)
    sum_ref[0:1, :] += jnp.sum(keys_b.astype(F32), axis=0, keepdims=True)
    for i in range(width // block):
        cut = slice(i * block, (i + 1) * block)
        acc_ref[i] += lax.dot_general(
            keys_b[:, cut], vals_b[:, cut], (((0,), (0,)), ((), ())), preferred_element_type=F32
        )

    @pl.when(step == pl.num_programs(0) - 1)
    def _():
        own = same_block((block, block), head)
        parts = []
        for i in range(width // block):
            full = jnp.where(own, acc_ref[i], 0.0)
            small = full[:head]
            for h in range(1, block // head):
                small = small + full[h * head : (h + 1) * head]
            parts.append(small)
        state = jnp.concatenate(parts, axis=1)
        total = sum_ref[0:1, :]
        high = total.astype(BF).astype(F32)
        low = total - high
        lines = [row[:, 128 * i : 128 * (i + 1)] for row in (high, low) for i in range(width // 128)]
        rows = out_ref.shape[1]
        lines.append(jnp.zeros((rows - len(lines), 128), F32))
        cuts = [state[i : i + rows] for i in range(0, head, rows)]
        for copy in staged:
            copy.wait()
        out_ref[0] = jnp.concatenate(cuts + [jnp.concatenate(lines, axis=0)], axis=1).astype(BF)


def unpack(packed, head, width):
    rows = packed.shape[0]
    cuts = head // rows
    state = jnp.concatenate([packed[:, i * width : (i + 1) * width] for i in range(cuts)], axis=0)
    tail = packed[:, cuts * width :]
    lines = width // 128
    both = tail[:lines] + tail[lines : 2 * lines]
    return state, jnp.concatenate([both[i : i + 1] for i in range(lines)], axis=1)


def run_state(me, tokens, qkv_weight, out_weight, taps, head):
    count, width = tokens.shape
    steps, block = 4, 256
    rows = 16
    packed = head // rows * width + 128
    channels = taps.shape[1]
    return pl.pallas_call(
        functools.partial(state_kernel, head),
        grid=(steps,),
        in_specs=[
            pl.BlockSpec(memory_space=pltpu.SMEM),
            pl.BlockSpec((count // steps, width), lambda i: (i, 0)),
            pl.BlockSpec((width, width), lambda i: (0, 1)),
            pl.BlockSpec((width, width), lambda i: (0, 2)),
            HBM,
            HBM,
            HBM,
        ],
        out_specs=[pl.BlockSpec((1, rows, packed), lambda i: (0, 0, 0))] + [INSIDE] * 4,
        out_shape=[
            jax.ShapeDtypeStruct((1, rows, packed), BF),
            pltpu.VMEM((width, width), BF),
            pltpu.VMEM(out_weight.shape, BF),
            pltpu.VMEM((6 * channels, 2 * channels), BF),
            pltpu.VMEM((4 * channels, 2 * channels), BF),
        ],
        scratch_shapes=[
            pltpu.VMEM((width // block, block, block), F32),
            pltpu.VMEM((8, width), F32),
            pltpu.SemaphoreType.DMA((6,)),
        ],
        compiler_params=params(16),
        cost_estimate=cost(4 * count * width * width, 8 * count * width),
    )(me, tokens, qkv_weight, qkv_weight, qkv_weight, out_weight, taps)


def queries(tok, wq):
    return jnp.maximum(dot(tok, wq).astype(BF).astype(F32), 0.0)


def attend(qf, state, total, own, ones):
    block = own.shape[0]
    head, width = state.shape
    qb = qf.astype(BF)
    den_in = (qf * total).astype(BF)
    outs = []
    for i in range(width // block):
        cut = slice(i * block, (i + 1) * block)
        wide = jnp.concatenate([state[:, cut]] * (block // head), axis=0)
        wide = jnp.where(own, wide, jnp.zeros_like(wide))
        numer = dot(qb[:, cut], wide)
        denom = dot(den_in[:, cut], ones) + 1.0
        outs.append(numer / denom)
    return jnp.concatenate(outs, axis=1)


def valid_rows(first, limit, frames, rows):
    frame = lax.broadcasted_iota(jnp.int32, (frames * rows, 1), 0) // rows + first
    return frame < limit


def store_taps(x_ref, at, line, rows):
    m, channels = line.shape[0], line.shape[1] // 2
    column = lax.broadcasted_iota(jnp.int32, (m, 1), 0) % rows
    even_px, odd_px = line[:, :channels], line[:, channels:]
    left = jnp.where(column == 0, 0.0, pltpu.roll(odd_px, 1, 0))
    right = jnp.where(column == rows - 1, 0.0, pltpu.roll(even_px, m - 1, 0))
    for b, taps in enumerate(((left, even_px, odd_px), (even_px, odd_px, right))):
        for d, tap in enumerate(taps):
            cut = slice(at + d * channels, at + (d + 1) * channels)
            x_ref[b * m : (b + 1) * m, cut] = tap.astype(BF)


def line_taps(line, rows):
    m, channels = line.shape[0], line.shape[1] // 2
    column = lax.broadcasted_iota(jnp.int32, (m, 1), 0) % rows
    even_px, odd_px = line[:, :channels], line[:, channels:]
    left = jnp.where(column == 0, 0.0, pltpu.roll(odd_px, 1, 0))
    right = jnp.where(column == rows - 1, 0.0, pltpu.roll(even_px, m - 1, 0))
    return jnp.concatenate([left.astype(BF), line.astype(BF), right.astype(BF)], axis=1)


def gather_stats(run_ref, res, live, limit, first, frames, rows):
    part = jnp.sum(res, axis=0, keepdims=True)
    count = (jnp.clip(limit - first, 0, frames) * (2 * rows)).astype(F32)
    mean = part / jnp.maximum(count, 1.0)
    dev = jnp.where(live, res - mean, 0.0)
    spread = jnp.sum(dev * dev, axis=0, keepdims=True)
    had = (jnp.clip(limit, 0, first) * (2 * rows)).astype(F32)
    run_sum = run_ref[0:1, :]
    gap = mean - run_sum / jnp.maximum(had, 1.0)
    weight = had * count / jnp.maximum(had + count, 1.0)
    run_ref[1:2, :] += spread + gap * gap * weight
    run_ref[0:1, :] = run_sum + part


def near_kernel(
    rows, parts, frames, pos_ref, group_ref, valid_ref, *refs
):
    pieces, refs = refs[: 2 * parts], refs[2 * parts :]
    own_any, inner_any, wq_ref, wo_ref, w2_ref, taps_hbm, *refs = refs
    near_ref, part_ref, state_ref, total_ref, stat_ref, *refs = refs
    acc_ref, pend_ref, att_ref, x_ref, w1_ref, own_ref, inner_ref, buf_ref, *refs = refs
    own_sem, inner_sem, piece_sem, sems = refs
    late = spread_row(taps_hbm, 2 - 2 * jnp.bitwise_and(pos_ref[0], 1), w1_ref, sems)
    step = pl.program_id(0)
    count, width = own_ref.shape
    m = frames * rows
    steps = count // m
    me = pos_ref[0]
    odd = jnp.bitwise_and(me, 1)
    head = state_ref.shape[1]
    channels = near_ref.shape[2]
    size = pieces[0].shape[0]
    fetch = [
        pltpu.make_async_copy(
            pieces[i], buf_ref.at[i // parts, pl.ds(i % parts * size, size)], piece_sem.at[i]
        )
        for i in range(2 * parts)
    ]

    @pl.when(step == 0)
    def _():
        for copy in fetch:
            copy.start()
        for i in range(steps):
            chunk(own_any, own_ref, i, m, own_sem).start()
            chunk(inner_any, inner_ref, i, m, inner_sem).start()
        for copy in late:
            copy.start()
        clear_spread(w1_ref)
        acc_ref[...] = jnp.zeros_like(acc_ref)
        pend_ref[...] = jnp.zeros_like(pend_ref)
        stat_ref[...] = jnp.zeros_like(stat_ref)
        for copy in fetch:
            copy.wait()

    chunk(own_any, own_ref, step, m, own_sem).wait()
    chunk(inner_any, inner_ref, step, m, inner_sem).wait()
    here = pl.ds(pl.multiple_of(step * m, m), m)
    block = 256
    own = same_block((block, block), head)
    ones = jnp.where(own, 1.0, 0.0).astype(BF)
    wq = wq_ref[...]
    q_own = queries(own_ref[here, :], wq)
    q_inner = queries(inner_ref[here, :], wq)
    for i in range(frames):
        frame = step * frames + i
        rel = jnp.bitwise_xor(frame, me)
        piece = buf_ref[jnp.bitwise_and(rel, 1), rel // 2].astype(F32)
        before = group_ref[jnp.maximum(frame - 1, 0)]
        fresh = jnp.where(group_ref[frame] != before, 1.0, 0.0)
        pend = pend_ref[...]
        acc = acc_ref[...] + fresh * pend
        acc_ref[...] = acc
        pend_ref[...] = (1.0 - fresh) * pend + piece
        summed = acc + piece
        state, total = unpack(summed, head, width)
        state = state.astype(BF)
        state_ref[frame] = state
        total_ref[frame] = jnp.broadcast_to(total, (8, width))
        cut = slice(i * rows, (i + 1) * rows)
        both = jnp.concatenate([q_own[cut], q_inner[cut]], axis=0)
        res = attend(both, state, total, own, ones)
        att_ref[0, cut] = res[:rows]
        att_ref[1, cut] = res[rows:]
    first = step * frames
    limit = valid_ref[me]
    keep_own = valid_rows(first, limit, frames, rows)
    keep_inner = valid_rows(first, valid_ref[jnp.bitwise_xor(me, 1)], frames, rows)

    @pl.when(step == 0)
    def _():
        for copy in late:
            copy.wait()

    half, row = 2 * channels, 3 * channels
    mine = jnp.where(keep_own, dot(att_ref[0].astype(BF), wo_ref[...]), 0.0)
    w_close = wo_ref[:, pl.ds(pl.multiple_of(odd * half, half), half)]
    close = jnp.where(keep_inner, dot(att_ref[1].astype(BF), w_close), 0.0)
    store_taps(x_ref, 0, mine[:, : 2 * channels], rows)
    store_taps(x_ref, row, mine[:, 2 * channels :], rows)
    live = jnp.concatenate([keep_own, keep_own], axis=0)
    pair = dot(x_ref[...], w2_ref[...])
    more = dot(line_taps(close, rows), w1_ref[...])
    more = jnp.concatenate([more[:, :channels], more[:, channels:]], axis=0)
    res = jnp.where(live, pair[:, :channels] + more, 0.0)
    near_ref[0, here] = res[:m]
    near_ref[1, here] = res[m:]
    gather_stats(stat_ref, res, live, limit, first, frames, rows)
    part_ref[0, here] = pair[:m, channels:]
    part_ref[1, here] = pair[m:, channels:]


def near(rows, me, group_map, valid, pieces, own, inner, weights, channels, head):
    count, width = own.shape
    frames = 16
    n = count // rows
    m = frames * rows
    deep, packed = pieces[0].shape[1:]
    parts = len(pieces) // 2
    return pl.pallas_call(
        functools.partial(near_kernel, rows, parts, frames),
        grid_spec=pltpu.PrefetchScalarGridSpec(
            num_scalar_prefetch=3,
            grid=(n // frames,),
            in_specs=[ANY] * (2 * parts + 2) + [INSIDE] * 3 + [HBM],
            out_specs=[INSIDE] * 5,
            scratch_shapes=[
                pltpu.VMEM((deep, packed), F32),
                pltpu.VMEM((deep, packed), F32),
                pltpu.VMEM((2, m, width), F32),
                pltpu.VMEM((2 * m, 6 * channels), BF),
                pltpu.VMEM((4 * channels, 2 * channels), BF),
                pltpu.VMEM((count, width), BF),
                pltpu.VMEM((count, width), BF),
                pltpu.VMEM((2, n // 2, deep, packed), BF),
                pltpu.SemaphoreType.DMA((n // frames,)),
                pltpu.SemaphoreType.DMA((n // frames,)),
                pltpu.SemaphoreType.DMA((2 * parts,)),
                pltpu.SemaphoreType.DMA((2,)),
            ],
        ),
        out_shape=[
            pltpu.VMEM((2, count, channels), F32),
            pltpu.VMEM((2, count, channels), F32),
            pltpu.VMEM((n, head, width), BF),
            pltpu.VMEM((n, 8, width), F32),
            pltpu.VMEM((8, channels), F32),
        ],
        compiler_params=params(32),
        cost_estimate=cost(1, 1),
    )(me, group_map, valid, *pieces, own, inner, *weights)


def far_kernel(
    rows, first, last, pos_ref, valid_ref,
    outer_any, state_ref, total_ref, part_ref, before_ref, near_stat_ref, wq_ref, wo_ref, wx_ref,
    far_ref, stat_ref,
    att_ref, run_ref, outer_ref, sem,
):
    m, width = outer_ref.shape
    channels = far_ref.shape[2]
    frames = m // rows
    me = pos_ref[0]
    odd = jnp.bitwise_and(me, 1)
    head = state_ref.shape[1]
    half = 2 * channels
    half_at = pl.ds(pl.multiple_of((1 - odd) * half, half), half)
    copy = pltpu.make_async_copy(outer_any, outer_ref, sem)
    copy.start()
    run_ref[...] = before_ref[...]
    block = 256
    own = same_block((block, block), head)
    ones = jnp.where(own, 1.0, 0.0).astype(BF)
    copy.wait()
    qf = queries(outer_ref[...], wq_ref[...])
    for i in range(frames):
        cut = slice(i * rows, (i + 1) * rows)
        frame = first + i
        att_ref[cut] = attend(qf[cut], state_ref[frame], total_ref[frame][0:1], own, ones)
    outer_at = jnp.clip(me + 2 * odd - 1, 0, valid_ref.shape[0] - 1)
    keep = valid_rows(first, valid_ref[outer_at], frames, rows)
    line = jnp.where(keep, dot(att_ref[...].astype(BF), wo_ref[:, half_at]), 0.0)
    more = dot(line_taps(line, rows), wx_ref[...])
    more = jnp.concatenate([more[:, :channels], more[:, channels:]], axis=0)
    limit = valid_ref[me]
    live = valid_rows(first, limit, frames, rows)
    live = jnp.concatenate([live, live], axis=0)
    here = pl.ds(first * rows, m)
    part = jnp.concatenate([part_ref[0, here], part_ref[1, here]], axis=0)
    res = jnp.where(live, part + more, 0.0)
    far_ref[0] = res[:m]
    far_ref[1] = res[m:]
    gather_stats(run_ref, res, live, limit, first, frames, rows)
    if last:
        both = jnp.concatenate([near_stat_ref[0:2], run_ref[0:2], run_ref[4:8]], axis=0)
        stat_ref[...] = jnp.broadcast_to(both[None], stat_ref.shape)
    else:
        stat_ref[...] = run_ref[...]


def far(rows, first, me, valid, outer, state, total, part, before, near_stat, weights):
    m, width = outer.shape
    channels = part.shape[2]
    n = state.shape[0]
    last = first + m // rows == n
    smem = pl.BlockSpec(memory_space=pltpu.SMEM)
    stat = jax.ShapeDtypeStruct((n, 8, channels), F32) if last else pltpu.VMEM((8, channels), F32)
    return pl.pallas_call(
        functools.partial(far_kernel, rows, first, last),
        in_specs=[smem, smem, ANY] + [INSIDE] * 8,
        out_specs=[INSIDE, INSIDE],
        scratch_shapes=[
            pltpu.VMEM((m, width), F32),
            pltpu.VMEM((8, channels), F32),
            pltpu.VMEM((m, width), BF),
            pltpu.SemaphoreType.DMA,
        ],
        out_shape=[pltpu.VMEM((2, m, channels), F32), stat],
        compiler_params=pltpu.CompilerParams(vmem_limit_bytes=16 * MIB),
        cost_estimate=cost(1, 1),
    )(me, valid, outer, state, total, part, before, near_stat, *weights)


def norm_kernel(
    rows, size, frames, pos_ref, valid_ref, stat_ref, gain_ref, bias_ref, near_ref, far0_ref, far1_ref,
    out_hbm, mix_ref, out_ref, sems,
):
    m = frames * rows
    channels = out_ref.shape[3]
    me = pos_ref[0]
    odd = jnp.bitwise_and(me, 1)

    stat = stat_ref[...]
    tile = lax.broadcasted_iota(jnp.int32, (stat.shape[0], channels), 0)
    counts = jnp.zeros(tile.shape, F32)
    for i in range(stat.shape[0]):
        counts = jnp.where(tile == i, (valid_ref[i] * (2 * rows)).astype(F32), counts)
    mix = jnp.where(same_block((channels, channels), size), 1.0, 0.0)
    all_count = jnp.sum(counts, axis=0, keepdims=True) * (2 * size)

    def grouped(row):
        wide = jnp.broadcast_to(row, (8, channels))
        return dot(wide, mix, precision=lax.Precision.HIGHEST)[0:1]

    sums = stat[:, 0, :] + stat[:, 2, :]
    mean = grouped(jnp.sum(sums, axis=0, keepdims=True)) / all_count
    gap0 = stat[:, 0, :] / counts - mean
    gap1 = stat[:, 2, :] / counts - mean
    spread = stat[:, 1, :] + stat[:, 3, :] + (gap0 * gap0 + gap1 * gap1) * counts
    var = grouped(jnp.sum(spread, axis=0, keepdims=True)) / all_count
    scale = gain_ref[...] * lax.rsqrt(var + 1e-5)
    mul = 0.5 * scale
    add = 0.5 * (bias_ref[...] - mean * scale)
    stores = []
    for step in range(valid_ref.shape[0] // frames):
        live = valid_rows(step * frames, valid_ref[me], frames, rows)
        here = pl.ds(step * m, m)
        cut = far0_ref.shape[1]
        there = pl.ds(step * m % cut, m)
        late_ref = far1_ref if step * m >= cut else far0_ref
        for y in range(2):
            line = 1 - odd if y == 0 else odd
            for b in range(2):
                if y == 0:
                    half = near_ref[b, here] * mul + add
                else:
                    half = late_ref[b, there] * mul + add
                z = jnp.where(live, half + half * jnp.tanh(half), 0.0)
                for c in range(channels // 128):
                    mix_ref[y, c, pl.ds(b, m, 2), :] = z[:, 128 * c : 128 * (c + 1)]
            for f in range(frames):
                for c in range(channels // 128):
                    out_ref[step * frames + f, line, :, 128 * c : 128 * (c + 1)] = mix_ref[
                        y, c, 2 * rows * f : 2 * rows * (f + 1), :
                    ].astype(BF)
        now = pl.ds(step * frames, frames)
        stores.append(pltpu.make_async_copy(out_ref.at[now], out_hbm.at[now], sems.at[step]))
        stores[-1].start()
    for copy in stores:
        copy.wait()


def norm(rows, me, valid, stat, gain, bias, near_plane, *far_planes):
    count, channels = near_plane.shape[1:]
    n = valid.shape[0]
    frames = n // 4
    m = frames * rows
    smem = pl.BlockSpec(memory_space=pltpu.SMEM)
    return pl.pallas_call(
        functools.partial(norm_kernel, rows, channels // NORM_GROUPS, frames),
        in_specs=[smem, smem] + [INSIDE] * 6,
        out_specs=HBM,
        scratch_shapes=[
            pltpu.VMEM((2, channels // 128, 2 * m + 8, 128), F32),
            pltpu.VMEM((n, 2, 2 * rows, channels), BF),
            pltpu.SemaphoreType.DMA((n // frames,)),
        ],
        out_shape=pltpu.HBM((n, 2, 2 * rows, channels), BF),
        compiler_params=pltpu.CompilerParams(vmem_limit_bytes=24 * MIB),
        cost_estimate=cost(32 * count * channels, 24 * count * channels, 4 * count * channels),
    )(
        me, valid, stat, gain.reshape(1, channels), bias.reshape(1, channels), near_plane, *far_planes
    )


def local(
    tokens,
    qkv_weight,
    out_weight,
    conv_weight,
    norm_gain,
    norm_bias,
    group_map,
    token_order,
    valid_frames,
):
    tiles = lax.axis_size("tm")
    rank = lax.axis_index("tm")
    count, width = tokens.shape
    rows = count // tiles
    channels = conv_weight.shape[3]
    head = width // HEADS
    me = rank.reshape(1).astype(jnp.int32)

    def swap(x, pairs):
        return lax.ppermute(x, "tm", pairs)

    qkv_weight, out_weight, taps = (
        pltpu.with_memory_space_constraint(w, pltpu.HBM)
        for w in (qkv_weight, out_weight, conv_weight.reshape(-1, channels))
    )
    raster = permute(token_order, tokens)
    tile = lax.all_to_all(
        raster.reshape(tiles, rows, width), "tm", split_axis=0, concat_axis=0, tiled=True
    ).reshape(count, width)
    buf, wq, wo, w2, wx = run_state(me, tokens, qkv_weight, out_weight, taps, head)

    def swap_by(x, k):
        return swap(x, [(i, i ^ k) for i in range(tiles)])

    k, gate = 2, None
    while k < tiles:
        ks = [k] if k == 2 or 2 * k >= tiles else [k, 2 * k, 3 * k]
        got = [swap_by(buf, j) for j in ks]
        gate = got[0]
        buf = jnp.concatenate([buf] + got, axis=0)
        k *= 2 if len(ks) == 1 else 4
    pieces = [buf, swap_by(buf, 1)]
    tile, _ = lax.optimization_barrier((tile, gate))
    inner = swap_by(tile, 1)
    ends = [(i, i + 1) for i in range(1, tiles - 1, 2)]
    ends = ends + [(j, i) for i, j in ends]
    cut = count // 4 * 3
    outer = [swap(tile[:cut], ends), swap(tile[cut:], ends)]
    near_plane, part, state, total, near_stat = near(
        rows, me, group_map, valid_frames, pieces, tile, inner, (wq, wo, w2, taps),
        channels, head,
    )
    stat, planes = jnp.zeros((8, channels), F32), []
    for i, piece in enumerate(outer):
        plane, stat = far(
            rows, i * cut // rows, me, valid_frames, piece, state, total, part, stat, near_stat,
            (wq, wo, wx),
        )
        planes.append(plane)
    stat = lax.all_to_all(stat, "tm", split_axis=0, concat_axis=0, tiled=True)
    return norm(rows, me, valid_frames, stat, norm_gain, norm_bias, near_plane, *planes)


def solution(mesh):
    in_specs = (P(("clip", "tm"), None), P(), P(), P(), P(), P(), P("clip"), P("clip"), P("clip"))
    out_specs = P("clip", "tm", None, None)
    return jax.shard_map(local, mesh=mesh, in_specs=in_specs, out_specs=out_specs, check_vma=False)
```
